32 devices in a mesh: tomo: 8 (over z, y), cls: 4 (over x, core).
Axes of the slice: x: 2, y: 2, z: 4, core: 2. Of those that a mesh axis runs over, the one named last changes fastest.
Arguments:
- particles: bfloat16 [256, 64, 4096], P(('tomo', 'cls')), may hold values from -6 to 6
- inverse_noise: float32 [256], P(('tomo', 'cls')), may hold values from 0.005 to 0.04
- tomogram: int32 [256], P(('tomo', 'cls')), may hold values from 0 to 31, as said below
- candidates: int32 [256, 4], P(('tomo', 'cls')), may hold values from 0 to 31, as said below
- rotations: int32 [256, 8], P(('tomo', 'cls')), may hold values from 0 to 15, as said below
- wedge: int32 [32, 32, 32], P('tomo'), may hold values from 0 to 1
- references: bfloat16 [32, 16, 65536], P('cls'), may hold values from -8 to 8
Outputs:
- posterior: float32 [256, 32], P(('tomo', 'cls'))
- class_sums: float32 [32, 16, 65536], P('cls', None, 'tomo')
- wedge_sums: float32 [32, 16, 1024], P('cls', None, 'tomo')
The draws below stay inside these ranges and needn't reach their ends.
Inputs may be any that keep to these rules, and one draw needn't show every extreme that they name: The tomogram of a particle held by index t of tomo is one of t * 4 to t * 4 + 3. `candidates`: each particle lists 4 different classes: two held by each of two different indices of cls (class c is held by index c // 8). Of the 8 particles of one device, at most 4 list classes of any one index of cls, and in every row of tomo one index of cls is listed by exactly 4 particles of every device of that row. `rotations`: 8 different indices for each particle.
All inputs are finite; a program needn't handle non-finite values.
Results may differ from the reference program's by a relative error of at most 0.009.
Values may be sent and summed in bfloat16 or wider, within the bound.
A program may use at most 256 MiB of HBM per device.

```python
import math
import jax
import jax.numpy as jnp
from jax import lax

VOX = 64
KB = 32
CLASSES = 32
NSET = 16
ROT = 8
CAND = 4
PART_DEV = 8
TOMO_DEV = 4
CLS_DEV = 8
PARTICLES = 256
TOMOGRAMS = 32


def volume_of(key, particle_index):
    gaussian = jax.random.normal(jax.random.fold_in(jax.random.fold_in(key, 303), particle_index), (VOX, VOX * VOX), jnp.float32)
    return jnp.clip(gaussian, -6.0, 6.0).astype(jnp.bfloat16)


def candidate_table(key):
    owners = CLASSES // CLS_DEV
    spread = owners - 1
    blocks = PARTICLES // PART_DEV
    row_count = blocks // owners
    capacity = PART_DEV // 2
    sub_keys = jax.random.split(jax.random.fold_in(key, 101), 6)
    hottest = jax.random.randint(sub_keys[0], (row_count,), 0, owners, dtype=jnp.int32)
    hot_block = jnp.repeat(hottest, owners)
    shuffle = jax.vmap(lambda sub_key: jax.random.permutation(sub_key, spread))(jax.random.split(sub_keys[1], blocks)).astype(jnp.int32)
    others = (hot_block[:, None] + 1 + shuffle) % owners
    position = jnp.arange(PART_DEV, dtype=jnp.int32)
    hit_first = jnp.where(position < capacity, position, capacity + 2 * (position - capacity))
    pick_first = jnp.take_along_axis(others, jnp.broadcast_to(hit_first % spread, (blocks, PART_DEV)), axis=1)
    first_owner = jnp.where(position[None, :] < capacity, hot_block[:, None], pick_first)
    hit_second = jnp.where(position < capacity, position, hit_first + 1) % spread
    second_owner = jnp.take_along_axis(others, jnp.broadcast_to(hit_second, (blocks, PART_DEV)), axis=1)
    reorder = jax.vmap(lambda sub_key: jax.random.permutation(sub_key, PART_DEV))(jax.random.split(sub_keys[2], blocks)).astype(jnp.int32)
    first_owner = jnp.take_along_axis(first_owner, reorder, axis=1)
    second_owner = jnp.take_along_axis(second_owner, reorder, axis=1)
    first_pick = jax.random.randint(sub_keys[3], (blocks, PART_DEV, 2), 0, CLS_DEV, dtype=jnp.int32)
    second_pick = (first_pick + 1 + jax.random.randint(sub_keys[4], (blocks, PART_DEV, 2), 0, CLS_DEV - 1, dtype=jnp.int32)) % CLS_DEV
    listed = jnp.stack([first_owner * CLS_DEV + first_pick[..., 0], first_owner * CLS_DEV + second_pick[..., 0], second_owner * CLS_DEV + first_pick[..., 1], second_owner * CLS_DEV + second_pick[..., 1]], axis=-1).reshape(PARTICLES, CAND)
    mixing = jax.vmap(lambda sub_key: jax.random.permutation(sub_key, CAND))(jax.random.split(sub_keys[5], PARTICLES)).astype(jnp.int32)
    return jnp.take_along_axis(listed, mixing, axis=1).astype(jnp.int32)


def rotation_table(key):
    sub_keys = jax.random.split(jax.random.fold_in(key, 202), PARTICLES)
    return jax.vmap(lambda sub_key: jax.random.permutation(sub_key, NSET)[:ROT])(sub_keys).astype(jnp.int32)


def draw_particles(key, part):
    return lax.map(lambda particle_index: volume_of(key, particle_index), jnp.arange(PARTICLES, dtype=jnp.int32))


def draw_tomogram(key, part):
    row_total = TOMOGRAMS // TOMO_DEV
    per_row = PARTICLES // row_total
    row_of = jnp.arange(PARTICLES, dtype=jnp.int32) // per_row
    offset = jax.random.randint(jax.random.fold_in(key, 601), (PARTICLES,), 0, TOMO_DEV, dtype=jnp.int32)
    return (row_of * TOMO_DEV + offset).astype(jnp.int32)


def draw_candidates(key, part):
    return candidate_table(key)


def draw_rotations(key, part):
    return rotation_table(key)


def draw_wedge(key, part):
    upper_slopes = jax.random.randint(jax.random.fold_in(key, 701), (TOMOGRAMS,), 4, 4 * KB + 1, dtype=jnp.int32)
    lower_slopes = jax.random.randint(jax.random.fold_in(key, 702), (TOMOGRAMS,), 4, 4 * KB + 1, dtype=jnp.int32)
    signed = jnp.arange(KB, dtype=jnp.int32) - KB // 2
    magnitude = jnp.abs(signed)
    slope_rows = jnp.where(signed[None, :] >= 0, upper_slopes[:, None], lower_slopes[:, None])
    kept = 8 * magnitude[None, None, :] <= slope_rows[:, :, None] * magnitude[None, :, None]
    return kept.astype(jnp.int32)


def draw_references(key, part):
    gaussian = jax.random.normal(jax.random.fold_in(key, 404), (CLASSES, NSET, 2 * KB ** 3), jnp.float32)
    values = jnp.clip(gaussian, -8.0, 8.0) * 0.7071
    return values.astype(jnp.bfloat16)


def steps_of(stream_key, dims, cuts, low, largest):
    def one(axis_at, parts):
        heights = jax.random.uniform(jax.random.fold_in(jax.random.fold_in(stream_key, 6), axis_at), (parts,), jnp.float32, low / len(cuts), largest / len(cuts))
        return jnp.repeat(jnp.exp(heights), dims[axis_at] // parts).reshape((-1,) + (1,) * (len(dims) - axis_at - 1))

    loudness = one(*cuts[0])
    for cut in cuts[1:]:
        loudness = loudness * one(*cut)
    return loudness


def setup_inputs(seed: int = 0) -> dict:
    arg_keys = jax.random.split(jax.random.key(seed), 8)
    particles = draw_particles(jax.random.fold_in(arg_keys[7], 71), 0)
    inverse_noise = jnp.clip(jnp.exp(math.log(0.04) - 2.0794415 * jax.random.uniform(arg_keys[1], (PARTICLES,), jnp.float32) ** steps_of(arg_keys[1], (PARTICLES,), ((0, 32),), -0.2, 0.2)), 0.005, 0.04)
    tomogram = draw_tomogram(jax.random.fold_in(arg_keys[7], 71), 0)
    candidates = draw_candidates(jax.random.fold_in(arg_keys[7], 71), 0)
    rotations = draw_rotations(jax.random.fold_in(arg_keys[7], 71), 0)
    wedge = draw_wedge(jax.random.fold_in(arg_keys[7], 71), 0)
    references = draw_references(jax.random.fold_in(arg_keys[7], 71), 0)
    return dict(particles=particles, inverse_noise=inverse_noise, tomogram=tomogram, candidates=candidates, rotations=rotations, wedge=wedge, references=references)


HIGHEST = lax.Precision.HIGHEST


def band_spectrum(volume):
    cube = volume.astype(jnp.float32).reshape(VOX, VOX, VOX)
    full = jnp.fft.fftn(cube) / (VOX ** 1.5)
    picks = (jnp.arange(KB) - KB // 2) % VOX
    band_part = full[picks][:, picks][:, :, picks]
    return jnp.stack([jnp.real(band_part), jnp.imag(band_part)])


def reference(particles, inverse_noise, tomogram, candidates, rotations, wedge, references):
    wedge_rows = wedge.reshape(TOMOGRAMS, KB * KB).astype(jnp.float32)
    particle_masks = wedge_rows[tomogram]
    spectra = lax.map(band_spectrum, particles).astype(jnp.bfloat16)
    masked = spectra * particle_masks.reshape(PARTICLES, 1, KB, 1, KB).astype(jnp.bfloat16)
    masked = masked.reshape(PARTICLES, 2 * KB ** 3)
    flat_refs = references.reshape(CLASSES * NSET, 2 * KB ** 3)
    ref_values = references.astype(jnp.float32).reshape(CLASSES * NSET, 2, KB, KB, KB)
    power = jnp.sum(ref_values * ref_values, axis=(1, 3)).reshape(CLASSES * NSET, KB * KB)
    quadratic = jnp.dot(power, wedge_rows.T, precision=HIGHEST)
    pair_codes = candidates[:, :, None] * NSET + rotations[:, None, :]
    penalty = quadratic[pair_codes, tomogram[:, None, None]]
    blocks = PARTICLES // PART_DEV
    block_spec = masked.reshape(blocks, PART_DEV, 2 * KB ** 3)
    block_codes = pair_codes.reshape(blocks, PART_DEV, CAND * ROT)

    def inner_block(pieces):
        spec_piece, code_piece = pieces
        chosen = flat_refs[code_piece.reshape(-1)].reshape(PART_DEV, CAND * ROT, 2 * KB ** 3)
        return jnp.einsum("bq,bhq->bh", spec_piece.astype(jnp.float32), chosen.astype(jnp.float32), precision=HIGHEST)

    inner = lax.map(inner_block, (block_spec, block_codes)).reshape(PARTICLES, CAND, ROT)
    raw = inner - 0.5 * penalty
    logits = inverse_noise[:, None] * raw.reshape(PARTICLES, CAND * ROT)
    posterior = jax.nn.softmax(logits, axis=-1)
    rounded = lax.optimization_barrier(posterior.astype(jnp.bfloat16)).astype(jnp.float32)
    block_weights = rounded.reshape(blocks, PART_DEV, CAND * ROT)
    block_masks = particle_masks.reshape(blocks, PART_DEV, KB * KB)

    def add_block(totals, pieces):
        class_total, wedge_total = totals
        spec_piece, code_piece, weight_piece, mask_piece = pieces
        flat_codes = code_piece.reshape(-1)
        class_terms = weight_piece[:, :, None] * spec_piece.astype(jnp.float32)[:, None, :]
        wedge_terms = weight_piece[:, :, None] * mask_piece[:, None, :]
        class_total = class_total.at[flat_codes].add(class_terms.reshape(PART_DEV * CAND * ROT, 2 * KB ** 3))
        wedge_total = wedge_total.at[flat_codes].add(wedge_terms.reshape(PART_DEV * CAND * ROT, KB * KB))
        return (class_total, wedge_total), None

    start_totals = (jnp.zeros((CLASSES * NSET, 2 * KB ** 3), jnp.float32), jnp.zeros((CLASSES * NSET, KB * KB), jnp.float32))
    (class_total, wedge_total), _ = lax.scan(add_block, start_totals, (block_spec, block_codes, block_weights, block_masks))
    return posterior, class_total.reshape(CLASSES, NSET, 2 * KB ** 3), wedge_total.reshape(CLASSES, NSET, KB * KB)
```

```python
import functools
import math

import jax
import jax.numpy as jnp
import ml_dtypes
import numpy as np
from jax import lax
from jax.experimental import pallas as pl
from jax.experimental.pallas import tpu as pltpu
from jax.sharding import PartitionSpec as P

KB = 32
NSET = 16
ROT = 8
CAND = 4
LANES = 128
MESH = pl.DeviceIdType.MESH
BF16 = jnp.bfloat16
F32 = jnp.float32
HIGHEST = lax.Precision.HIGHEST
VMEM_LIMIT = 56 * 1024 * 1024


def split_table(table):
    high = table.astype(ml_dtypes.bfloat16)
    low = (table - high.astype(np.float64)).astype(ml_dtypes.bfloat16)
    return high, low


def dft_table(length):
    frequency = np.arange(KB) - KB // 2
    radians = np.mod(np.outer(frequency, np.arange(length)), length) * (2.0 * math.pi / length)
    return np.exp(-1j * radians) / math.sqrt(length)


@functools.lru_cache(maxsize=None)
def plane_tables(length):
    one = dft_table(length)
    plane = np.einsum("jy,kz->yzjk", one, one).reshape(length * length, KB * KB // LANES, LANES)
    both = np.stack([plane.real, plane.imag], axis=2).reshape(length * length, 2 * KB * KB)
    return split_table(both)


@functools.lru_cache(maxsize=None)
def depth_tables(length, part_count, tomo_axis):
    blocks = tomo_axis // 2
    per_block = KB // blocks
    half = per_block // 2
    one = dft_table(length)
    big = np.zeros((2, blocks, half, 2, part_count, part_count, length))
    for block in range(blocks):
        for k in range(half):
            for h in range(2):
                row = one[block * per_block + h * half + k]
                for p in range(part_count):
                    big[0, block, k, h, p, p] = row.real
                    big[1, block, k, h, p, p] = row.imag
    return split_table(big.reshape(2 * KB * part_count, part_count * length))


def dot(a, b):
    return jnp.dot(a, b, preferred_element_type=F32)


def dft_kernel(blocks, half, x_ref, th_ref, tl_ref, wh_ref, wl_ref, mask_ref, out_ref):
    tile = pl.program_id(0)
    values = x_ref[...]
    plane = dot(values, th_ref[...]) + dot(values, tl_ref[...])
    high = plane.astype(BF16)
    low = (plane - high.astype(F32)).astype(BF16)
    wide = dot(wh_ref[...], high) + dot(wh_ref[...], low) + dot(wl_ref[...], high)
    rows = wide.shape[0] // 2
    mask = mask_ref[...]
    real = (wide[:rows, :LANES] - wide[rows:, LANES:]) * mask
    imag = (wide[:rows, LANES:] + wide[rows:, :LANES]) * mask
    group = rows // (blocks * half)
    for a, part in enumerate((real.astype(BF16), imag.astype(BF16))):
        for block in range(blocks):
            for k in range(half):
                start = (block * half + k) * group
                column = pl.multiple_of(k * KB * KB + tile * LANES, LANES)
                out_ref[a * blocks + block, :, pl.ds(column, LANES)] = part[start : start + group]


def spectra_chunks(particles, mask_rows, tomo_axis):
    part_count, length, plane_size = particles.shape
    blocks = tomo_axis // 2
    half = KB // blocks // 2
    width = half * KB * KB
    th, tl = plane_tables(length)
    wh, wl = depth_tables(length, part_count, tomo_axis)
    tiles = KB * KB // LANES
    whole = lambda shape: pl.BlockSpec(shape, lambda j: (0,) * len(shape))
    return pl.pallas_call(
        functools.partial(dft_kernel, blocks, half),
        grid=(tiles,),
        out_shape=jax.ShapeDtypeStruct((tomo_axis, 2 * part_count, width), BF16),
        in_specs=[
            whole((part_count * length, plane_size)),
            pl.BlockSpec((plane_size, 2 * LANES), lambda j: (0, j)),
            pl.BlockSpec((plane_size, 2 * LANES), lambda j: (0, j)),
            whole(wh.shape),
            whole(wl.shape),
            whole(mask_rows.shape),
        ],
        out_specs=whole((tomo_axis, 2 * part_count, width)),
        compiler_params=pltpu.CompilerParams(vmem_limit_bytes=VMEM_LIMIT),
        name="dft",
    )(
        particles.reshape(part_count * length, plane_size),
        jnp.asarray(th),
        jnp.asarray(tl),
        jnp.asarray(wh),
        jnp.asarray(wl),
        mask_rows,
    )


def exchange_kernel(tomo_axis, cls_axis, m_ref, out_ref, local_sem, s1, r1, sx, rx, sc, rc):
    me_t, me_c = lax.axis_index("tomo"), lax.axis_index("cls")
    x_axis = cls_axis // 2
    xi, core = me_c // 2, me_c % 2
    sibling = xi * 2 + 1 - core

    def x_peer(d):
        return lax.rem(xi + d, x_axis) * 2 + core

    def x_source(d):
        return lax.rem(xi + x_axis - d, x_axis)

    def copy(src, slot, device, send, recv):
        return pltpu.make_async_remote_copy(
            src_ref=src,
            dst_ref=out_ref.at[slot],
            send_sem=send,
            recv_sem=recv,
            device_id=device,
            device_id_type=MESH,
        )

    barrier = pltpu.get_barrier_semaphore()
    peers = [(lax.rem(me_t + k, tomo_axis), me_c) for k in range(1, tomo_axis)]
    peers += [(me_t, x_peer(d)) for d in range(1, x_axis)]
    peers += [(me_t, sibling)]
    for device in peers:
        pl.semaphore_signal(barrier, inc=1, device_id=device, device_id_type=MESH)
    pl.semaphore_wait(barrier, len(peers))

    mine = me_t * cls_axis + me_c
    own = pltpu.make_async_copy(m_ref.at[me_t], out_ref.at[mine], local_sem)
    own.start()
    sends = []
    for k in range(1, tomo_axis):
        target = lax.rem(me_t + k, tomo_axis)
        one = copy(m_ref.at[target], mine, (target, me_c), s1.at[k], r1.at[k])
        one.start()
        sends.append(one)
    for k in range(tomo_axis):
        source = lax.rem(me_t + tomo_axis - k, tomo_axis)
        slot = source * cls_axis + me_c
        if k == 0:
            own.wait()
        else:
            copy(m_ref.at[0], slot, (source, me_c), s1.at[k], r1.at[k]).wait_recv()
        for d in range(1, x_axis):
            one = copy(out_ref.at[slot], slot, (me_t, x_peer(d)), sx.at[d, k], rx.at[d, k])
            one.start()
            sends.append(one)
        one = copy(out_ref.at[slot], slot, (me_t, sibling), sc.at[0, k], rc.at[0, k])
        one.start()
        sends.append(one)
    for k in range(tomo_axis):
        source = lax.rem(me_t + tomo_axis - k, tomo_axis)
        for d in range(1, x_axis):
            slot = source * cls_axis + x_source(d) * 2 + core
            copy(out_ref.at[slot], slot, (me_t, x_peer(d)), sx.at[d, k], rx.at[d, k]).wait_recv()
            one = copy(out_ref.at[slot], slot, (me_t, sibling), sc.at[d, k], rc.at[d, k])
            one.start()
            sends.append(one)
    for k in range(tomo_axis):
        source = lax.rem(me_t + tomo_axis - k, tomo_axis)
        for d in range(x_axis):
            slot = source * cls_axis + x_source(d) * 2 + 1 - core
            copy(out_ref.at[slot], slot, (me_t, sibling), sc.at[d, k], rc.at[d, k]).wait_recv()
    for one in sends:
        one.wait_send()


def exchange(chunks, tomo_axis, cls_axis):
    x_axis = cls_axis // 2
    dma = pltpu.SemaphoreType.DMA
    return pl.pallas_call(
        functools.partial(exchange_kernel, tomo_axis, cls_axis),
        out_shape=jax.ShapeDtypeStruct((tomo_axis * cls_axis,) + chunks.shape[1:], BF16),
        in_specs=[pl.BlockSpec(memory_space=pl.ANY)],
        out_specs=pl.BlockSpec(memory_space=pl.ANY),
        scratch_shapes=[
            dma,
            dma((tomo_axis,)),
            dma((tomo_axis,)),
            dma((x_axis, tomo_axis)),
            dma((x_axis, tomo_axis)),
            dma((x_axis, tomo_axis)),
            dma((x_axis, tomo_axis)),
        ],
        compiler_params=pltpu.CompilerParams(collective_id=1, has_side_effects=True),
        name="exchange",
    )(chunks)


def score_kernel(place_ref, slots_ref, refs_ref, wedge_ref, codes_ref, out_ref, acc, pen):
    h = pl.program_id(0)
    refs = refs_ref[...]
    products = lax.dot_general(
        slots_ref[...], refs, (((1,), (1,)), ((), ())), preferred_element_type=F32
    )
    rows, wide = products.shape
    paired = products.reshape(rows // 16, 16, wide)
    inner = jnp.where(h == 0, paired[:, :8], paired[:, 8:]).reshape(rows // 2, wide)
    pieces = []
    plane = KB * KB
    for k in range(refs.shape[1] // plane):
        total = None
        for j in range(plane // LANES):
            start = k * plane + j * LANES
            piece = refs[:, start : start + LANES].astype(F32)
            square = piece * piece
            total = square if total is None else total + square
        pieces.append(total)
    power = jnp.concatenate(pieces, axis=1)
    penalty = lax.dot_general(
        wedge_ref[...].astype(F32),
        power,
        (((1,), (1,)), ((), ())),
        preferred_element_type=F32,
        precision=HIGHEST,
    )

    @pl.when(h == 0)
    def _():
        acc[...] = inner
        pen[...] = penalty

    @pl.when(h == 1)
    def _():
        codes = codes_ref[...]
        tomos = pen.shape[0]
        hot = codes[:, CAND * ROT : CAND * ROT + 1] == lax.broadcasted_iota(
            jnp.int32, (rows // 2, tomos), 1
        )
        chosen = jnp.dot(
            hot.astype(F32), pen[...] + penalty, preferred_element_type=F32, precision=HIGHEST
        )
        raw = acc[...] + inner - 0.5 * chosen
        local = codes - place_ref[1]
        lane = lax.broadcasted_iota(jnp.int32, codes.shape, 1)
        valid = (local >= 0) & (local < wide) & (lane < CAND * ROT)
        picked = jnp.take_along_axis(raw, jnp.where(valid, local, 0), axis=1)
        out_ref[...] = jnp.where(valid, picked, 0.0)


def scores(place, slots, refs, wedge_block, codes):
    rows, width = slots.shape
    tomos = wedge_block.shape[0]
    depth = wedge_block.shape[1] // 2
    wide = refs.shape[0]
    return pl.pallas_call(
        score_kernel,
        grid_spec=pltpu.PrefetchScalarGridSpec(
            num_scalar_prefetch=1,
            grid=(2,),
            in_specs=[
                pl.BlockSpec((rows, width), lambda h, place: (0, 0)),
                pl.BlockSpec((wide, width), lambda h, place: (0, 2 * place[0] + h)),
                pl.BlockSpec((tomos, depth), lambda h, place: (0, h)),
                pl.BlockSpec(codes.shape, lambda h, place: (0, 0)),
            ],
            out_specs=pl.BlockSpec(codes.shape, lambda h, place: (0, 0)),
            scratch_shapes=[
                pltpu.VMEM((rows // 2, wide), F32),
                pltpu.VMEM((tomos, wide), F32),
            ],
        ),
        out_shape=jax.ShapeDtypeStruct(codes.shape, F32),
        compiler_params=pltpu.CompilerParams(vmem_limit_bytes=VMEM_LIMIT),
        name="scores",
    )(place, slots, refs, wedge_block, codes)


def weights_kernel(
    tomo_axis, cls_axis, part_ref, noise_ref, post_ref, all_ref, own, land, s1, r1, s2, r2
):
    count = tomo_axis * cls_axis
    me_t, me_c = lax.axis_index("tomo"), lax.axis_index("cls")
    me = me_t * cls_axis + me_c

    def place(index):
        return (index // cls_axis, lax.rem(index, cls_axis))

    barrier = pltpu.get_barrier_semaphore()

    def greet(k, carry):
        pl.semaphore_signal(
            barrier, inc=1, device_id=place(lax.rem(me + k, count)), device_id_type=MESH
        )
        return carry

    lax.fori_loop(1, count, greet, 0)
    pl.semaphore_wait(barrier, count - 1)

    def first(k):
        target = lax.rem(me + k, count)
        return pltpu.make_async_remote_copy(
            src_ref=part_ref.at[target],
            dst_ref=land.at[k],
            send_sem=s1.at[k],
            recv_sem=r1.at[k],
            device_id=place(target),
            device_id_type=MESH,
        )

    def second(k):
        target = lax.rem(me + k, count)
        return pltpu.make_async_remote_copy(
            src_ref=own,
            dst_ref=all_ref.at[me],
            send_sem=s2.at[k],
            recv_sem=r2.at[k],
            device_id=place(target),
            device_id_type=MESH,
        )

    def arrived(k):
        source = lax.rem(me + count - k, count)
        return pltpu.make_async_remote_copy(
            src_ref=own,
            dst_ref=all_ref.at[source],
            send_sem=s2.at[k],
            recv_sem=r2.at[k],
            device_id=place(source),
            device_id_type=MESH,
        )

    def run(step):
        def loop(k, carry):
            step(k)
            return carry

        lax.fori_loop(1, count, loop, 0)

    run(lambda k: first(k).start())
    land[0] = part_ref[me]
    run(lambda k: first(k).wait_recv())
    raw = jnp.sum(land[...], axis=0)
    lane = lax.broadcasted_iota(jnp.int32, raw.shape, 1)
    logits = jnp.where(lane < CAND * ROT, raw * noise_ref[...], -jnp.inf)
    top = jnp.max(logits, axis=1, keepdims=True)
    grown = jnp.exp(logits - top)
    posterior = grown / jnp.sum(grown, axis=1, keepdims=True)
    post_ref[...] = posterior
    rounded = posterior.astype(BF16).astype(F32)
    own[...] = rounded
    run(lambda k: second(k).start())
    all_ref[me] = rounded
    run(lambda k: arrived(k).wait_recv())
    run(lambda k: first(k).wait_send())
    run(lambda k: second(k).wait_send())


def weights(partial, noise, tomo_axis, cls_axis):
    count = tomo_axis * cls_axis
    dma = pltpu.SemaphoreType.DMA
    tile = partial.shape[1:]
    return pl.pallas_call(
        functools.partial(weights_kernel, tomo_axis, cls_axis),
        out_shape=(
            jax.ShapeDtypeStruct(tile, F32),
            jax.ShapeDtypeStruct(partial.shape, F32),
        ),
        in_specs=[pl.BlockSpec(memory_space=pltpu.VMEM)] * 2,
        out_specs=(pl.BlockSpec(memory_space=pltpu.VMEM),) * 2,
        scratch_shapes=[pltpu.VMEM(tile, F32), pltpu.VMEM(partial.shape, F32)]
        + [dma((count,))] * 4,
        compiler_params=pltpu.CompilerParams(collective_id=2, has_side_effects=True),
        name="weights",
    )(partial, noise)


def sums_kernel(place_ref, slots_ref, codes_ref, weights_ref, wedge_ref, class_ref, wsum_ref, table):
    h, tile = pl.program_id(0), pl.program_id(1)
    particles = codes_ref.shape[0]
    wide = class_ref.shape[0]

    @pl.when((h == 0) & (tile == 0))
    def _():
        local = codes_ref[...] - place_ref[1]
        value = weights_ref[...]
        lane = lax.broadcasted_iota(jnp.int32, (particles, wide), 1)
        total = jnp.zeros((particles, wide), F32)
        for k in range(CAND * ROT):
            total += jnp.where(local[:, k : k + 1] == lane, value[:, k : k + 1], 0.0)
        zero = jnp.zeros((particles // 8, 8, wide), F32)
        stacked = total.reshape(particles // 8, 8, wide)
        first = jnp.concatenate([stacked, zero], axis=1).reshape(2 * particles, wide)
        second = jnp.concatenate([zero, stacked], axis=1).reshape(2 * particles, wide)
        table[0] = first.T.astype(BF16)
        table[1] = second.T.astype(BF16)
        tomos = wedge_ref.shape[0]
        hot = codes_ref[:, CAND * ROT : CAND * ROT + 1] == lax.broadcasted_iota(
            jnp.int32, (particles, tomos), 1
        )
        masks = dot(hot.astype(F32).astype(BF16), wedge_ref[...]).astype(BF16)
        wsum_ref[...] = dot(total.T.astype(BF16), masks)

    class_ref[...] = dot(table[h], slots_ref[...])


def sums(place, slots, codes, all_weights, wedge_columns, wide):
    rows, width = slots.shape
    tiles = 2
    step = width // tiles
    return pl.pallas_call(
        sums_kernel,
        grid_spec=pltpu.PrefetchScalarGridSpec(
            num_scalar_prefetch=1,
            grid=(2, tiles),
            in_specs=[
                pl.BlockSpec((rows, step), lambda h, i, place: (0, i)),
                pl.BlockSpec(codes.shape, lambda h, i, place: (0, 0)),
                pl.BlockSpec(all_weights.shape, lambda h, i, place: (0, 0)),
                pl.BlockSpec(wedge_columns.shape, lambda h, i, place: (0, 0)),
            ],
            out_specs=[
                pl.BlockSpec((wide, step), lambda h, i, place: (0, h * tiles + i)),
                pl.BlockSpec((wide, wedge_columns.shape[1]), lambda h, i, place: (0, 0)),
            ],
            scratch_shapes=[pltpu.VMEM((2, wide, rows), BF16)],
        ),
        out_shape=(
            jax.ShapeDtypeStruct((wide, 2 * width), F32),
            jax.ShapeDtypeStruct((wide, wedge_columns.shape[1]), F32),
        ),
        compiler_params=pltpu.CompilerParams(vmem_limit_bytes=VMEM_LIMIT),
        name="sums",
    )(place, slots, codes, all_weights, wedge_columns)


def body(
    tomo_axis,
    cls_axis,
    particles,
    inverse_noise,
    tomogram,
    candidates,
    rotations,
    wedge,
    references,
):
    part_count = particles.shape[0]
    class_count = references.shape[0]
    tomo_count = wedge.shape[0]
    wide = class_count * NSET
    blocks = tomo_axis // 2
    per_block = KB // blocks
    half = per_block // 2
    here = lax.axis_index("tomo")
    class_base = lax.axis_index("cls") * wide
    place = jnp.stack([here, class_base]).astype(jnp.int32)

    pair_codes = (candidates[:, :, None] * NSET + rotations[:, None, :]).reshape(part_count, -1)
    code_rows = jnp.concatenate(
        [
            pair_codes,
            tomogram[:, None],
            jnp.zeros((part_count, LANES - CAND * ROT - 1), jnp.int32),
        ],
        axis=1,
    )
    codes = lax.all_gather(code_rows, ("tomo", "cls"), axis=0, tiled=True)
    wedge_rows = lax.all_gather(
        wedge.reshape(tomo_count, KB * KB).astype(BF16), "tomo", axis=0, tiled=True
    )

    local_hot = (
        (tomogram - here * tomo_count)[:, None] == jnp.arange(tomo_count, dtype=jnp.int32)[None, :]
    ).astype(F32)
    own_masks = jnp.dot(local_hot, wedge.reshape(tomo_count, KB * KB).astype(F32))
    own_masks = own_masks.reshape(part_count, blocks, 2, half, KB).transpose(1, 3, 2, 0, 4)
    mask_rows = jnp.tile(own_masks.reshape(KB * part_count, KB), (1, LANES // KB))

    chunks = spectra_chunks(particles, mask_rows, tomo_axis)
    slots = exchange(chunks, tomo_axis, cls_axis)
    slots = slots.reshape(-1, slots.shape[-1])

    total_tomos = wedge_rows.shape[0]
    wedge_block = lax.dynamic_slice_in_dim(
        wedge_rows, lax.rem(here, blocks) * (per_block * KB), per_block * KB, 1
    ).reshape(total_tomos, per_block, 1, KB)
    wedge_block = jnp.broadcast_to(
        wedge_block, (total_tomos, per_block, LANES // KB, KB)
    ).reshape(total_tomos, per_block * LANES)
    flat_refs = references.reshape(wide, -1)
    partial = scores(place, slots, flat_refs, wedge_block, codes)
    noise = jnp.broadcast_to(inverse_noise[:, None], (part_count, LANES))
    posterior, all_weights = weights(
        partial.reshape(-1, part_count, LANES), noise, tomo_axis, cls_axis
    )
    columns = KB * KB // tomo_axis
    wedge_columns = lax.dynamic_slice_in_dim(wedge_rows, here * columns, columns, 1)
    class_flat, wedge_flat = sums(
        place, slots, codes, all_weights.reshape(-1, LANES), wedge_columns, wide
    )
    return (
        posterior[:, : CAND * ROT],
        class_flat.reshape(class_count, NSET, -1),
        wedge_flat.reshape(class_count, NSET, columns),
    )


def solution(mesh):
    return jax.shard_map(
        functools.partial(body, mesh.shape["tomo"], mesh.shape["cls"]),
        mesh=mesh,
        in_specs=(
            P(("tomo", "cls"), None, None),
            P(("tomo", "cls")),
            P(("tomo", "cls")),
            P(("tomo", "cls"), None),
            P(("tomo", "cls"), None),
            P("tomo", None, None),
            P("cls", None, None),
        ),
        out_specs=(P(("tomo", "cls"), None), P("cls", None, "tomo"), P("cls", None, "tomo")),
        check_vma=False,
    )
```

```python
import functools
import math

import jax
import jax.numpy as jnp
import ml_dtypes
import numpy as np
from jax import lax
from jax.experimental import pallas as pl
from jax.experimental.pallas import tpu as pltpu
from jax.sharding import PartitionSpec as P

KB = 32
NSET = 16
ROT = 8
CAND = 4
LANES = 128
MESH = pl.DeviceIdType.MESH
BF16 = jnp.bfloat16
F32 = jnp.float32
HIGHEST = lax.Precision.HIGHEST
VMEM_LIMIT = 56 * 1024 * 1024


def split_table(table):
    high = table.astype(ml_dtypes.bfloat16)
    low = (table - high.astype(np.float64)).astype(ml_dtypes.bfloat16)
    return high, low


def dft_table(length):
    frequency = np.arange(KB) - KB // 2
    radians = np.mod(np.outer(frequency, np.arange(length)), length) * (2.0 * math.pi / length)
    return np.exp(-1j * radians) / math.sqrt(length)


@functools.lru_cache(maxsize=None)
def plane_tables(length):
    one = dft_table(length)
    plane = np.einsum("jy,kz->yzjk", one, one).reshape(length * length, KB * KB // LANES, LANES)
    both = np.stack([plane.real, plane.imag], axis=2).reshape(length * length, 2 * KB * KB)
    return split_table(both)


@functools.lru_cache(maxsize=None)
def depth_tables(length, part_count, tomo_axis):
    blocks = tomo_axis // 2
    per_block = KB // blocks
    half = per_block // 2
    one = dft_table(length)
    big = np.zeros((2, blocks, half, 2, part_count, part_count, length))
    for block in range(blocks):
        for k in range(half):
            for h in range(2):
                row = one[block * per_block + h * half + k]
                for p in range(part_count):
                    big[0, block, k, h, p, p] = row.real
                    big[1, block, k, h, p, p] = row.imag
    return split_table(big.reshape(2 * KB * part_count, part_count * length))


def dot(a, b):
    return jnp.dot(a, b, preferred_element_type=F32)


def dft_kernel(blocks, half, x_ref, th_ref, tl_ref, wh_ref, wl_ref, mask_ref, out_ref):
    tile = pl.program_id(0)
    values = x_ref[...]
    plane = dot(values, th_ref[...]) + dot(values, tl_ref[...])
    high = plane.astype(BF16)
    low = (plane - high.astype(F32)).astype(BF16)
    wide = dot(wh_ref[...], high) + dot(wh_ref[...], low) + dot(wl_ref[...], high)
    rows = wide.shape[0] // 2
    mask = mask_ref[...]
    real = (wide[:rows, :LANES] - wide[rows:, LANES:]) * mask
    imag = (wide[:rows, LANES:] + wide[rows:, :LANES]) * mask
    group = rows // (blocks * half)
    for a, part in enumerate((real.astype(BF16), imag.astype(BF16))):
        for block in range(blocks):
            for k in range(half):
                start = (block * half + k) * group
                column = pl.multiple_of(k * KB * KB + tile * LANES, LANES)
                out_ref[a * blocks + block, :, pl.ds(column, LANES)] = part[start : start + group]


def spectra_chunks(particles, mask_rows, tomo_axis):
    part_count, length, plane_size = particles.shape
    blocks = tomo_axis // 2
    half = KB // blocks // 2
    width = half * KB * KB
    th, tl = plane_tables(length)
    wh, wl = depth_tables(length, part_count, tomo_axis)
    tiles = KB * KB // LANES
    whole = lambda shape: pl.BlockSpec(shape, lambda j: (0,) * len(shape))
    return pl.pallas_call(
        functools.partial(dft_kernel, blocks, half),
        grid=(tiles,),
        out_shape=jax.ShapeDtypeStruct((tomo_axis, 2 * part_count, width), BF16),
        in_specs=[
            whole((part_count * length, plane_size)),
            pl.BlockSpec((plane_size, 2 * LANES), lambda j: (0, j)),
            pl.BlockSpec((plane_size, 2 * LANES), lambda j: (0, j)),
            whole(wh.shape),
            whole(wl.shape),
            whole(mask_rows.shape),
        ],
        out_specs=whole((tomo_axis, 2 * part_count, width)),
        compiler_params=pltpu.CompilerParams(vmem_limit_bytes=VMEM_LIMIT),
        name="dft",
    )(
        particles.reshape(part_count * length, plane_size),
        jnp.asarray(th),
        jnp.asarray(tl),
        jnp.asarray(wh),
        jnp.asarray(wl),
        mask_rows,
    )


def exchange_kernel(
    tomo_axis,
    cls_axis,
    m_ref,
    code_ref,
    wedge_ref,
    out_ref,
    codes_ref,
    wedges_ref,
    local_sem,
    s1,
    r1,
    sx,
    rx,
    sc,
    rc,
    sk,
    rk,
    sw,
    rw,
):
    count = tomo_axis * cls_axis
    me_t, me_c = lax.axis_index("tomo"), lax.axis_index("cls")
    x_axis = cls_axis // 2
    xi, core = me_c // 2, me_c % 2
    sibling = xi * 2 + 1 - core

    def x_peer(d):
        return lax.rem(xi + d, x_axis) * 2 + core

    def x_source(d):
        return lax.rem(xi + x_axis - d, x_axis)

    def copy(src, slot, device, send, recv):
        return pltpu.make_async_remote_copy(
            src_ref=src,
            dst_ref=out_ref.at[slot],
            send_sem=send,
            recv_sem=recv,
            device_id=device,
            device_id_type=MESH,
        )

    mine = me_t * cls_axis + me_c

    def device_of(index):
        return (index // cls_axis, lax.rem(index, cls_axis))

    def code_copy(k, slot, device):
        return pltpu.make_async_remote_copy(
            src_ref=code_ref,
            dst_ref=codes_ref.at[slot],
            send_sem=sk.at[k],
            recv_sem=rk.at[k],
            device_id=device,
            device_id_type=MESH,
        )

    def wedge_copy(k, slot, device):
        return pltpu.make_async_remote_copy(
            src_ref=wedge_ref,
            dst_ref=wedges_ref.at[slot],
            send_sem=sw.at[k],
            recv_sem=rw.at[k],
            device_id=device,
            device_id_type=MESH,
        )

    def run(low, high, step):
        def loop(k, carry):
            step(k)
            return carry

        lax.fori_loop(low, high, loop, 0)

    barrier = pltpu.get_barrier_semaphore()
    run(
        1,
        count,
        lambda k: pl.semaphore_signal(
            barrier, inc=1, device_id=device_of(lax.rem(mine + k, count)), device_id_type=MESH
        ),
    )
    pl.semaphore_wait(barrier, count - 1)

    own = pltpu.make_async_copy(m_ref.at[me_t], out_ref.at[mine], local_sem.at[0])
    own.start()
    own_codes = pltpu.make_async_copy(code_ref, codes_ref.at[mine], local_sem.at[1])
    own_codes.start()
    own_wedge = pltpu.make_async_copy(wedge_ref, wedges_ref.at[me_t], local_sem.at[2])
    own_wedge.start()
    sends = []
    for k in range(1, tomo_axis):
        target = lax.rem(me_t + k, tomo_axis)
        one = copy(m_ref.at[target], mine, (target, me_c), s1.at[k], r1.at[k])
        one.start()
        sends.append(one)
    for k in range(1, tomo_axis):
        one = wedge_copy(k, me_t, (lax.rem(me_t + k, tomo_axis), me_c))
        one.start()
        sends.append(one)
    run(1, count, lambda k: code_copy(k, mine, device_of(lax.rem(mine + k, count))).start())
    for k in range(tomo_axis):
        source = lax.rem(me_t + tomo_axis - k, tomo_axis)
        slot = source * cls_axis + me_c
        if k == 0:
            own.wait()
        else:
            copy(m_ref.at[0], slot, (source, me_c), s1.at[k], r1.at[k]).wait_recv()
        for d in range(1, x_axis):
            one = copy(out_ref.at[slot], slot, (me_t, x_peer(d)), sx.at[d, k], rx.at[d, k])
            one.start()
            sends.append(one)
        one = copy(out_ref.at[slot], slot, (me_t, sibling), sc.at[0, k], rc.at[0, k])
        one.start()
        sends.append(one)
    for k in range(tomo_axis):
        source = lax.rem(me_t + tomo_axis - k, tomo_axis)
        for d in range(1, x_axis):
            slot = source * cls_axis + x_source(d) * 2 + core
            copy(out_ref.at[slot], slot, (me_t, x_peer(d)), sx.at[d, k], rx.at[d, k]).wait_recv()
            one = copy(out_ref.at[slot], slot, (me_t, sibling), sc.at[d, k], rc.at[d, k])
            one.start()
            sends.append(one)
    for k in range(tomo_axis):
        source = lax.rem(me_t + tomo_axis - k, tomo_axis)
        for d in range(x_axis):
            slot = source * cls_axis + x_source(d) * 2 + 1 - core
            copy(out_ref.at[slot], slot, (me_t, sibling), sc.at[d, k], rc.at[d, k]).wait_recv()
    own_codes.wait()
    own_wedge.wait()
    for k in range(1, tomo_axis):
        source = lax.rem(me_t + tomo_axis - k, tomo_axis)
        wedge_copy(k, source, (source, me_c)).wait_recv()

    def code_arrived(k):
        source = lax.rem(mine + count - k, count)
        code_copy(k, source, device_of(source)).wait_recv()

    run(1, count, code_arrived)
    run(1, count, lambda k: code_copy(k, mine, device_of(lax.rem(mine + k, count))).wait_send())
    for one in sends:
        one.wait_send()


def exchange(chunks, code_rows, wedge_own, tomo_axis, cls_axis):
    count = tomo_axis * cls_axis
    x_axis = cls_axis // 2
    dma = pltpu.SemaphoreType.DMA
    return pl.pallas_call(
        functools.partial(exchange_kernel, tomo_axis, cls_axis),
        out_shape=(
            jax.ShapeDtypeStruct((count,) + chunks.shape[1:], BF16),
            jax.ShapeDtypeStruct((count,) + code_rows.shape, jnp.int32),
            jax.ShapeDtypeStruct((tomo_axis,) + wedge_own.shape, BF16),
        ),
        in_specs=[pl.BlockSpec(memory_space=pl.ANY)] * 3,
        out_specs=(pl.BlockSpec(memory_space=pl.ANY),) * 3,
        scratch_shapes=[
            dma((3,)),
            dma((tomo_axis,)),
            dma((tomo_axis,)),
            dma((x_axis, tomo_axis)),
            dma((x_axis, tomo_axis)),
            dma((x_axis, tomo_axis)),
            dma((x_axis, tomo_axis)),
            dma((count,)),
            dma((count,)),
            dma((tomo_axis,)),
            dma((tomo_axis,)),
        ],
        compiler_params=pltpu.CompilerParams(collective_id=1, has_side_effects=True),
        name="exchange",
    )(chunks, code_rows, wedge_own)


def score_kernel(place_ref, slots_ref, refs_ref, wedge_ref, codes_ref, out_ref, acc, pen):
    h = pl.program_id(0)
    refs = refs_ref[...]
    products = lax.dot_general(
        slots_ref[...], refs, (((1,), (1,)), ((), ())), preferred_element_type=F32
    )
    rows, wide = products.shape
    paired = products.reshape(rows // 16, 16, wide)
    inner = jnp.where(h == 0, paired[:, :8], paired[:, 8:]).reshape(rows // 2, wide)
    pieces = []
    plane = KB * KB
    for k in range(refs.shape[1] // plane):
        total = None
        for j in range(plane // LANES):
            start = k * plane + j * LANES
            piece = refs[:, start : start + LANES].astype(F32)
            square = piece * piece
            total = square if total is None else total + square
        pieces.append(total)
    power = jnp.concatenate(pieces, axis=1)
    penalty = lax.dot_general(
        wedge_ref[...].astype(F32),
        power,
        (((1,), (1,)), ((), ())),
        preferred_element_type=F32,
        precision=HIGHEST,
    )

    @pl.when(h == 0)
    def _():
        acc[...] = inner
        pen[...] = penalty

    @pl.when(h == 1)
    def _():
        codes = codes_ref[...]
        tomos = pen.shape[0]
        hot = codes[:, CAND * ROT : CAND * ROT + 1] == lax.broadcasted_iota(
            jnp.int32, (rows // 2, tomos), 1
        )
        chosen = jnp.dot(
            hot.astype(F32), pen[...] + penalty, preferred_element_type=F32, precision=HIGHEST
        )
        raw = acc[...] + inner - 0.5 * chosen
        local = codes - place_ref[1]
        lane = lax.broadcasted_iota(jnp.int32, codes.shape, 1)
        valid = (local >= 0) & (local < wide) & (lane < CAND * ROT)
        picked = jnp.take_along_axis(raw, jnp.where(valid, local, 0), axis=1)
        out_ref[...] = jnp.where(valid, picked, 0.0)


def scores(place, slots, refs, wedge_block, codes):
    rows, width = slots.shape
    tomos = wedge_block.shape[0]
    depth = wedge_block.shape[1] // 2
    wide = refs.shape[0]
    return pl.pallas_call(
        score_kernel,
        grid_spec=pltpu.PrefetchScalarGridSpec(
            num_scalar_prefetch=1,
            grid=(2,),
            in_specs=[
                pl.BlockSpec((rows, width), lambda h, place: (0, 0)),
                pl.BlockSpec((wide, width), lambda h, place: (0, 2 * place[0] + h)),
                pl.BlockSpec((tomos, depth), lambda h, place: (0, h)),
                pl.BlockSpec(codes.shape, lambda h, place: (0, 0)),
            ],
            out_specs=pl.BlockSpec(codes.shape, lambda h, place: (0, 0)),
            scratch_shapes=[
                pltpu.VMEM((rows // 2, wide), F32),
                pltpu.VMEM((tomos, wide), F32),
            ],
        ),
        out_shape=jax.ShapeDtypeStruct(codes.shape, F32),
        compiler_params=pltpu.CompilerParams(vmem_limit_bytes=VMEM_LIMIT),
        name="scores",
    )(place, slots, refs, wedge_block, codes)


def weights_kernel(
    tomo_axis, cls_axis, part_ref, noise_ref, post_ref, all_ref, own, land, s1, r1, s2, r2
):
    count = tomo_axis * cls_axis
    me_t, me_c = lax.axis_index("tomo"), lax.axis_index("cls")
    me = me_t * cls_axis + me_c

    def place(index):
        return (index // cls_axis, lax.rem(index, cls_axis))

    barrier = pltpu.get_barrier_semaphore()

    def greet(k, carry):
        pl.semaphore_signal(
            barrier, inc=1, device_id=place(lax.rem(me + k, count)), device_id_type=MESH
        )
        return carry

    lax.fori_loop(1, count, greet, 0)
    pl.semaphore_wait(barrier, count - 1)

    def first(k):
        target = lax.rem(me + k, count)
        return pltpu.make_async_remote_copy(
            src_ref=part_ref.at[target],
            dst_ref=land.at[k],
            send_sem=s1.at[k],
            recv_sem=r1.at[k],
            device_id=place(target),
            device_id_type=MESH,
        )

    def second(k):
        target = lax.rem(me + k, count)
        return pltpu.make_async_remote_copy(
            src_ref=own,
            dst_ref=all_ref.at[me],
            send_sem=s2.at[k],
            recv_sem=r2.at[k],
            device_id=place(target),
            device_id_type=MESH,
        )

    def arrived(k):
        source = lax.rem(me + count - k, count)
        return pltpu.make_async_remote_copy(
            src_ref=own,
            dst_ref=all_ref.at[source],
            send_sem=s2.at[k],
            recv_sem=r2.at[k],
            device_id=place(source),
            device_id_type=MESH,
        )

    def run(step):
        def loop(k, carry):
            step(k)
            return carry

        lax.fori_loop(1, count, loop, 0)

    run(lambda k: first(k).start())
    land[0] = part_ref[me]
    run(lambda k: first(k).wait_recv())
    raw = jnp.sum(land[...], axis=0)
    lane = lax.broadcasted_iota(jnp.int32, raw.shape, 1)
    logits = jnp.where(lane < CAND * ROT, raw * noise_ref[...], -jnp.inf)
    top = jnp.max(logits, axis=1, keepdims=True)
    grown = jnp.exp(logits - top)
    posterior = grown / jnp.sum(grown, axis=1, keepdims=True)
    post_ref[...] = posterior
    rounded = posterior.astype(BF16).astype(F32)
    own[...] = rounded
    run(lambda k: second(k).start())
    all_ref[me] = rounded
    run(lambda k: arrived(k).wait_recv())
    run(lambda k: first(k).wait_send())
    run(lambda k: second(k).wait_send())


def weights(partial, noise, tomo_axis, cls_axis):
    count = tomo_axis * cls_axis
    dma = pltpu.SemaphoreType.DMA
    tile = partial.shape[1:]
    return pl.pallas_call(
        functools.partial(weights_kernel, tomo_axis, cls_axis),
        out_shape=(
            jax.ShapeDtypeStruct(tile, F32),
            jax.ShapeDtypeStruct(partial.shape, F32),
        ),
        in_specs=[pl.BlockSpec(memory_space=pltpu.VMEM)] * 2,
        out_specs=(pl.BlockSpec(memory_space=pltpu.VMEM),) * 2,
        scratch_shapes=[pltpu.VMEM(tile, F32), pltpu.VMEM(partial.shape, F32)]
        + [dma((count,))] * 4,
        compiler_params=pltpu.CompilerParams(collective_id=2, has_side_effects=True),
        name="weights",
    )(partial, noise)


def sums_kernel(place_ref, slots_ref, codes_ref, weights_ref, wedge_ref, class_ref, wsum_ref, table):
    h, tile = pl.program_id(0), pl.program_id(1)
    particles = codes_ref.shape[0]
    wide = class_ref.shape[0]

    @pl.when((h == 0) & (tile == 0))
    def _():
        local = codes_ref[...] - place_ref[1]
        value = weights_ref[...]
        lane = lax.broadcasted_iota(jnp.int32, (particles, wide), 1)
        total = jnp.zeros((particles, wide), F32)
        for k in range(CAND * ROT):
            total += jnp.where(local[:, k : k + 1] == lane, value[:, k : k + 1], 0.0)
        zero = jnp.zeros((particles // 8, 8, wide), F32)
        stacked = total.reshape(particles // 8, 8, wide)
        first = jnp.concatenate([stacked, zero], axis=1).reshape(2 * particles, wide)
        second = jnp.concatenate([zero, stacked], axis=1).reshape(2 * particles, wide)
        table[0] = first.T.astype(BF16)
        table[1] = second.T.astype(BF16)
        tomos = wedge_ref.shape[0]
        hot = codes_ref[:, CAND * ROT : CAND * ROT + 1] == lax.broadcasted_iota(
            jnp.int32, (particles, tomos), 1
        )
        masks = dot(hot.astype(F32).astype(BF16), wedge_ref[...]).astype(BF16)
        wsum_ref[...] = dot(total.T.astype(BF16), masks)

    class_ref[...] = dot(table[h], slots_ref[...])


def sums(place, slots, codes, all_weights, wedge_columns, wide):
    rows, width = slots.shape
    tiles = 2
    step = width // tiles
    return pl.pallas_call(
        sums_kernel,
        grid_spec=pltpu.PrefetchScalarGridSpec(
            num_scalar_prefetch=1,
            grid=(2, tiles),
            in_specs=[
                pl.BlockSpec((rows, step), lambda h, i, place: (0, i)),
                pl.BlockSpec(codes.shape, lambda h, i, place: (0, 0)),
                pl.BlockSpec(all_weights.shape, lambda h, i, place: (0, 0)),
                pl.BlockSpec(wedge_columns.shape, lambda h, i, place: (0, 0)),
            ],
            out_specs=[
                pl.BlockSpec((wide, step), lambda h, i, place: (0, h * tiles + i)),
                pl.BlockSpec((wide, wedge_columns.shape[1]), lambda h, i, place: (0, 0)),
            ],
            scratch_shapes=[pltpu.VMEM((2, wide, rows), BF16)],
        ),
        out_shape=(
            jax.ShapeDtypeStruct((wide, 2 * width), F32),
            jax.ShapeDtypeStruct((wide, wedge_columns.shape[1]), F32),
        ),
        compiler_params=pltpu.CompilerParams(vmem_limit_bytes=VMEM_LIMIT),
        name="sums",
    )(place, slots, codes, all_weights, wedge_columns)


def body(
    tomo_axis,
    cls_axis,
    particles,
    inverse_noise,
    tomogram,
    candidates,
    rotations,
    wedge,
    references,
):
    part_count = particles.shape[0]
    class_count = references.shape[0]
    tomo_count = wedge.shape[0]
    wide = class_count * NSET
    blocks = tomo_axis // 2
    per_block = KB // blocks
    half = per_block // 2
    here = lax.axis_index("tomo")
    class_base = lax.axis_index("cls") * wide
    place = jnp.stack([here, class_base]).astype(jnp.int32)

    pair_codes = (candidates[:, :, None] * NSET + rotations[:, None, :]).reshape(part_count, -1)
    code_rows = jnp.concatenate(
        [
            pair_codes,
            tomogram[:, None],
            jnp.zeros((part_count, LANES - CAND * ROT - 1), jnp.int32),
        ],
        axis=1,
    )
    local_hot = (
        (tomogram - here * tomo_count)[:, None] == jnp.arange(tomo_count, dtype=jnp.int32)[None, :]
    ).astype(F32)
    own_masks = jnp.dot(local_hot, wedge.reshape(tomo_count, KB * KB).astype(F32))
    own_masks = own_masks.reshape(part_count, blocks, 2, half, KB).transpose(1, 3, 2, 0, 4)
    mask_rows = jnp.tile(own_masks.reshape(KB * part_count, KB), (1, LANES // KB))

    chunks = spectra_chunks(particles, mask_rows, tomo_axis)
    wedge_own = wedge.reshape(-1, LANES).astype(BF16)
    slots, codes, wedge_rows = exchange(chunks, code_rows, wedge_own, tomo_axis, cls_axis)
    codes = codes.reshape(-1, LANES)
    wedge_rows = wedge_rows.reshape(-1, KB * KB)
    slots = slots.reshape(-1, slots.shape[-1])

    total_tomos = wedge_rows.shape[0]
    wedge_block = lax.dynamic_slice_in_dim(
        wedge_rows, lax.rem(here, blocks) * (per_block * KB), per_block * KB, 1
    ).reshape(total_tomos, per_block, 1, KB)
    wedge_block = jnp.broadcast_to(
        wedge_block, (total_tomos, per_block, LANES // KB, KB)
    ).reshape(total_tomos, per_block * LANES)
    flat_refs = references.reshape(wide, -1)
    partial = scores(place, slots, flat_refs, wedge_block, codes)
    noise = jnp.broadcast_to(inverse_noise[:, None], (part_count, LANES))
    posterior, all_weights = weights(
        partial.reshape(-1, part_count, LANES), noise, tomo_axis, cls_axis
    )
    columns = KB * KB // tomo_axis
    wedge_columns = lax.dynamic_slice_in_dim(wedge_rows, here * columns, columns, 1)
    class_flat, wedge_flat = sums(
        place, slots, codes, all_weights.reshape(-1, LANES), wedge_columns, wide
    )
    return (
        posterior[:, : CAND * ROT],
        class_flat.reshape(class_count, NSET, -1),
        wedge_flat.reshape(class_count, NSET, columns),
    )


def solution(mesh):
    return jax.shard_map(
        functools.partial(body, mesh.shape["tomo"], mesh.shape["cls"]),
        mesh=mesh,
        in_specs=(
            P(("tomo", "cls"), None, None),
            P(("tomo", "cls")),
            P(("tomo", "cls")),
            P(("tomo", "cls"), None),
            P(("tomo", "cls"), None),
            P("tomo", None, None),
            P("cls", None, None),
        ),
        out_specs=(P(("tomo", "cls"), None), P("cls", None, "tomo"), P("cls", None, "tomo")),
        check_vma=False,
    )
```

```python
import functools
import math

import jax
import jax.numpy as jnp
import ml_dtypes
import numpy as np
from jax import lax
from jax.experimental import pallas as pl
from jax.experimental.pallas import tpu as pltpu
from jax.sharding import PartitionSpec as P

KB = 32
NSET = 16
ROT = 8
CAND = 4
LANES = 128
GROUPS = 4
MESH = pl.DeviceIdType.MESH
BF16 = jnp.bfloat16
F32 = jnp.float32
HIGHEST = lax.Precision.HIGHEST
VMEM_LIMIT = 56 * 1024 * 1024


def split_table(table):
    high = table.astype(ml_dtypes.bfloat16)
    low = (table - high.astype(np.float64)).astype(ml_dtypes.bfloat16)
    return high, low


def dft_table(length):
    frequency = np.arange(KB) - KB // 2
    radians = np.mod(np.outer(frequency, np.arange(length)), length) * (2.0 * math.pi / length)
    return np.exp(-1j * radians) / math.sqrt(length)


@functools.lru_cache(maxsize=None)
def plane_tables(length):
    one = dft_table(length)
    plane = np.einsum("jy,kz->yzjk", one, one).reshape(length * length, KB * KB // LANES, LANES)
    both = np.stack([plane.real, plane.imag], axis=2).reshape(length * length, 2 * KB * KB)
    return split_table(both)


@functools.lru_cache(maxsize=None)
def depth_tables(length, part_count, tomo_axis):
    blocks = tomo_axis // 2
    per_block = KB // blocks
    half = per_block // 2
    one = dft_table(length)
    big = np.zeros((2, blocks, half, 2, part_count, part_count, length))
    for block in range(blocks):
        for k in range(half):
            for h in range(2):
                row = one[block * per_block + h * half + k]
                for p in range(part_count):
                    big[0, block, k, h, p, p] = row.real
                    big[1, block, k, h, p, p] = row.imag
    return split_table(big.reshape(2 * KB * part_count, part_count * length))


def dot(a, b):
    return jnp.dot(a, b, preferred_element_type=F32)


def spectra_kernel(
    tomo_axis,
    cls_axis,
    x_ref,
    th_ref,
    tl_ref,
    wh_ref,
    wl_ref,
    mask_ref,
    code_ref,
    wedge_ref,
    out_ref,
    codes_ref,
    wedges_ref,
    m_ref,
    local_sem,
    s1,
    r1,
    sx,
    rx,
    sc,
    rc,
    sk,
    rk,
    sw,
    rw,
):
    tile = pl.program_id(0)
    count = tomo_axis * cls_axis
    blocks = tomo_axis // 2
    half = KB // blocks // 2
    per_group = KB * KB // LANES // GROUPS
    lanes = per_group * LANES
    me_t, me_c = lax.axis_index("tomo"), lax.axis_index("cls")
    mine = me_t * cls_axis + me_c
    x_axis = cls_axis // 2
    xi, core = me_c // 2, me_c % 2
    sibling = (me_t, xi * 2 + 1 - core)

    def x_peer(d):
        return (me_t, lax.rem(xi + d, x_axis) * 2 + core)

    def x_source(d):
        return lax.rem(xi + x_axis - d, x_axis)

    def tomo_source(k):
        return lax.rem(me_t + tomo_axis - k, tomo_axis)

    def remote(src, dst, send, recv, device):
        return pltpu.make_async_remote_copy(
            src_ref=src,
            dst_ref=dst,
            send_sem=send,
            recv_sem=recv,
            device_id=device,
            device_id_type=MESH,
        )

    def device_of(index):
        return (index // cls_axis, lax.rem(index, cls_axis))

    def code_copy(k, slot, device):
        return remote(code_ref, codes_ref.at[slot], sk.at[k], rk.at[k], device)

    def wedge_copy(k, slot, device):
        return remote(wedge_ref, wedges_ref.at[slot], sw.at[k], rw.at[k], device)

    def first(g, k):
        target = lax.rem(me_t + k, tomo_axis)
        return remote(
            m_ref.at[g, target], out_ref.at[g, mine], s1.at[g, k], r1.at[g, k], (target, me_c)
        )

    def first_arrived(g, k):
        slot = tomo_source(k) * cls_axis + me_c
        return remote(
            m_ref.at[g, 0], out_ref.at[g, slot], s1.at[g, k], r1.at[g, k], (tomo_source(k), me_c)
        )

    def across(g, d, k, slot):
        here = out_ref.at[g, slot]
        return remote(here, here, sx.at[g, d, k], rx.at[g, d, k], x_peer(d))

    def over(g, d, k, slot):
        here = out_ref.at[g, slot]
        return remote(here, here, sc.at[g, d, k], rc.at[g, d, k], sibling)

    def own_copy(g):
        return pltpu.make_async_copy(m_ref.at[g, me_t], out_ref.at[g, mine], local_sem.at[g])

    def own_small():
        return (
            pltpu.make_async_copy(code_ref, codes_ref.at[mine], local_sem.at[GROUPS]),
            pltpu.make_async_copy(wedge_ref, wedges_ref.at[me_t], local_sem.at[GROUPS + 1]),
        )

    def run(low, high, step):
        def loop(k, carry):
            step(k)
            return carry

        lax.fori_loop(low, high, loop, 0)

    def send(g):
        own_copy(g).start()
        for k in range(1, tomo_axis):
            first(g, k).start()

    def forward(g):
        for k in range(tomo_axis):
            slot = tomo_source(k) * cls_axis + me_c
            if k == 0:
                own_copy(g).wait()
            else:
                first_arrived(g, k).wait_recv()
            for d in range(1, x_axis):
                across(g, d, k, slot).start()
            over(g, 0, k, slot).start()

    def share(g):
        for k in range(tomo_axis):
            for d in range(1, x_axis):
                slot = tomo_source(k) * cls_axis + x_source(d) * 2 + core
                across(g, d, k, slot).wait_recv()
                over(g, d, k, slot).start()

    @pl.when(tile == 0)
    def _():
        barrier = pltpu.get_barrier_semaphore()
        run(
            1,
            count,
            lambda k: pl.semaphore_signal(
                barrier, inc=1, device_id=device_of(lax.rem(mine + k, count)), device_id_type=MESH
            ),
        )
        pl.semaphore_wait(barrier, count - 1)
        for one in own_small():
            one.start()
        for k in range(1, tomo_axis):
            wedge_copy(k, me_t, (lax.rem(me_t + k, tomo_axis), me_c)).start()
        run(1, count, lambda k: code_copy(k, mine, device_of(lax.rem(mine + k, count))).start())

    values = x_ref[...]
    plane = dot(values, th_ref[...]) + dot(values, tl_ref[...])
    high = plane.astype(BF16)
    low = (plane - high.astype(F32)).astype(BF16)
    wide = dot(wh_ref[...], high) + dot(wh_ref[...], low) + dot(wl_ref[...], high)
    rows = wide.shape[0] // 2
    mask = mask_ref[...]
    real = (wide[:rows, :LANES] - wide[rows:, LANES:]) * mask
    imag = (wide[:rows, LANES:] + wide[rows:, :LANES]) * mask
    height = rows // (blocks * half)
    at = tile // per_group
    offset = lax.rem(tile, per_group) * LANES
    for a, part in enumerate((real.astype(BF16), imag.astype(BF16))):
        for block in range(blocks):
            for k in range(half):
                start = (block * half + k) * height
                column = pl.multiple_of(k * lanes + offset, LANES)
                m_ref[at, a * blocks + block, :, pl.ds(column, LANES)] = part[
                    start : start + height
                ]

    for g in range(GROUPS):

        @pl.when(tile == (g + 1) * per_group - 1)
        def _(g=g):
            send(g)
            if g >= 1:
                forward(g - 1)
            if g >= 2:
                share(g - 2)

    @pl.when(tile == GROUPS * per_group - 1)
    def _():
        if GROUPS >= 2:
            share(GROUPS - 2)
        forward(GROUPS - 1)
        share(GROUPS - 1)
        for g in range(GROUPS):
            for k in range(tomo_axis):
                for d in range(x_axis):
                    slot = tomo_source(k) * cls_axis + x_source(d) * 2 + 1 - core
                    over(g, d, k, slot).wait_recv()
        for one in own_small():
            one.wait()
        for k in range(1, tomo_axis):
            wedge_copy(k, tomo_source(k), (tomo_source(k), me_c)).wait_recv()

        def code_arrived(k):
            source = lax.rem(mine + count - k, count)
            code_copy(k, source, device_of(source)).wait_recv()

        run(1, count, code_arrived)
        run(1, count, lambda k: code_copy(k, mine, device_of(lax.rem(mine + k, count))).wait_send())
        for k in range(1, tomo_axis):
            wedge_copy(k, me_t, (lax.rem(me_t + k, tomo_axis), me_c)).wait_send()
        for g in range(GROUPS):
            for k in range(tomo_axis):
                if k:
                    first(g, k).wait_send()
                for d in range(x_axis):
                    slot = tomo_source(k) * cls_axis + x_source(d) * 2 + core
                    if d:
                        across(g, d, k, tomo_source(k) * cls_axis + me_c).wait_send()
                    over(g, d, k, slot).wait_send()


def spectra_slots(particles, mask_rows, code_rows, wedge_own, tomo_axis, cls_axis):
    part_count, length, plane_size = particles.shape
    count = tomo_axis * cls_axis
    x_axis = cls_axis // 2
    half = KB // tomo_axis
    piece = half * KB * KB // GROUPS
    th, tl = plane_tables(length)
    wh, wl = depth_tables(length, part_count, tomo_axis)
    tiles = KB * KB // LANES
    dma = pltpu.SemaphoreType.DMA
    whole = lambda shape: pl.BlockSpec(shape, lambda j: (0,) * len(shape))
    return pl.pallas_call(
        functools.partial(spectra_kernel, tomo_axis, cls_axis),
        grid=(tiles,),
        out_shape=(
            jax.ShapeDtypeStruct((GROUPS, count, 2 * part_count, piece), BF16),
            jax.ShapeDtypeStruct((count,) + code_rows.shape, jnp.int32),
            jax.ShapeDtypeStruct((tomo_axis,) + wedge_own.shape, BF16),
        ),
        in_specs=[
            whole((part_count * length, plane_size)),
            pl.BlockSpec((plane_size, 2 * LANES), lambda j: (0, j)),
            pl.BlockSpec((plane_size, 2 * LANES), lambda j: (0, j)),
            whole(wh.shape),
            whole(wl.shape),
            whole(mask_rows.shape),
            pl.BlockSpec(memory_space=pl.ANY),
            pl.BlockSpec(memory_space=pl.ANY),
        ],
        out_specs=(pl.BlockSpec(memory_space=pl.ANY),) * 3,
        scratch_shapes=[
            pltpu.VMEM((GROUPS, tomo_axis, 2 * part_count, piece), BF16),
            dma((GROUPS + 2,)),
            dma((GROUPS, tomo_axis)),
            dma((GROUPS, tomo_axis)),
            dma((GROUPS, x_axis, tomo_axis)),
            dma((GROUPS, x_axis, tomo_axis)),
            dma((GROUPS, x_axis, tomo_axis)),
            dma((GROUPS, x_axis, tomo_axis)),
            dma((count,)),
            dma((count,)),
            dma((tomo_axis,)),
            dma((tomo_axis,)),
        ],
        compiler_params=pltpu.CompilerParams(
            collective_id=1, has_side_effects=True, vmem_limit_bytes=VMEM_LIMIT
        ),
        name="spectra",
    )(
        particles.reshape(part_count * length, plane_size),
        jnp.asarray(th),
        jnp.asarray(tl),
        jnp.asarray(wh),
        jnp.asarray(wl),
        mask_rows,
        code_rows,
        wedge_own,
    )


def score_kernel(place_ref, slots_ref, refs_ref, wedge_ref, codes_ref, out_ref, acc, pen):
    h = pl.program_id(0)
    refs = refs_ref[...]
    products = None
    lanes = KB * KB // GROUPS
    for g in range(GROUPS):
        columns = jnp.concatenate(
            [
                refs[:, k * KB * KB + g * lanes : k * KB * KB + (g + 1) * lanes]
                for k in range(refs.shape[1] // (KB * KB))
            ],
            axis=1,
        )
        term = lax.dot_general(
            slots_ref[g], columns, (((1,), (1,)), ((), ())), preferred_element_type=F32
        )
        products = term if products is None else products + term
    rows, wide = products.shape
    paired = products.reshape(rows // 16, 16, wide)
    inner = jnp.where(h == 0, paired[:, :8], paired[:, 8:]).reshape(rows // 2, wide)
    pieces = []
    plane = KB * KB
    for k in range(refs.shape[1] // plane):
        total = None
        for j in range(plane // LANES):
            start = k * plane + j * LANES
            piece = refs[:, start : start + LANES].astype(F32)
            square = piece * piece
            total = square if total is None else total + square
        pieces.append(total)
    power = jnp.concatenate(pieces, axis=1)
    penalty = lax.dot_general(
        wedge_ref[...].astype(F32),
        power,
        (((1,), (1,)), ((), ())),
        preferred_element_type=F32,
        precision=HIGHEST,
    )

    @pl.when(h == 0)
    def _():
        acc[...] = inner
        pen[...] = penalty

    @pl.when(h == 1)
    def _():
        codes = codes_ref[...]
        tomos = pen.shape[0]
        hot = codes[:, CAND * ROT : CAND * ROT + 1] == lax.broadcasted_iota(
            jnp.int32, (rows // 2, tomos), 1
        )
        chosen = jnp.dot(
            hot.astype(F32), pen[...] + penalty, preferred_element_type=F32, precision=HIGHEST
        )
        raw = acc[...] + inner - 0.5 * chosen
        local = codes - place_ref[1]
        lane = lax.broadcasted_iota(jnp.int32, codes.shape, 1)
        valid = (local >= 0) & (local < wide) & (lane < CAND * ROT)
        picked = jnp.take_along_axis(raw, jnp.where(valid, local, 0), axis=1)
        out_ref[...] = jnp.where(valid, picked, 0.0)


def scores(place, slots, refs, wedge_block, codes):
    rows, width = slots.shape[1], slots.shape[2] * GROUPS
    tomos = wedge_block.shape[0]
    depth = wedge_block.shape[1] // 2
    wide = refs.shape[0]
    return pl.pallas_call(
        score_kernel,
        grid_spec=pltpu.PrefetchScalarGridSpec(
            num_scalar_prefetch=1,
            grid=(2,),
            in_specs=[
                pl.BlockSpec(slots.shape, lambda h, place: (0, 0, 0)),
                pl.BlockSpec((wide, width), lambda h, place: (0, 2 * place[0] + h)),
                pl.BlockSpec((tomos, depth), lambda h, place: (0, h)),
                pl.BlockSpec(codes.shape, lambda h, place: (0, 0)),
            ],
            out_specs=pl.BlockSpec(codes.shape, lambda h, place: (0, 0)),
            scratch_shapes=[
                pltpu.VMEM((rows // 2, wide), F32),
                pltpu.VMEM((tomos, wide), F32),
            ],
        ),
        out_shape=jax.ShapeDtypeStruct(codes.shape, F32),
        compiler_params=pltpu.CompilerParams(vmem_limit_bytes=VMEM_LIMIT),
        name="scores",
    )(place, slots, refs, wedge_block, codes)


def weights_kernel(
    tomo_axis, cls_axis, part_ref, noise_ref, post_ref, all_ref, own, land, s1, r1, s2, r2
):
    count = tomo_axis * cls_axis
    me_t, me_c = lax.axis_index("tomo"), lax.axis_index("cls")
    me = me_t * cls_axis + me_c

    def place(index):
        return (index // cls_axis, lax.rem(index, cls_axis))

    barrier = pltpu.get_barrier_semaphore()

    def greet(k, carry):
        pl.semaphore_signal(
            barrier, inc=1, device_id=place(lax.rem(me + k, count)), device_id_type=MESH
        )
        return carry

    lax.fori_loop(1, count, greet, 0)
    pl.semaphore_wait(barrier, count - 1)

    def first(k):
        target = lax.rem(me + k, count)
        return pltpu.make_async_remote_copy(
            src_ref=part_ref.at[target],
            dst_ref=land.at[k],
            send_sem=s1.at[k],
            recv_sem=r1.at[k],
            device_id=place(target),
            device_id_type=MESH,
        )

    def second(k):
        target = lax.rem(me + k, count)
        return pltpu.make_async_remote_copy(
            src_ref=own,
            dst_ref=all_ref.at[me],
            send_sem=s2.at[k],
            recv_sem=r2.at[k],
            device_id=place(target),
            device_id_type=MESH,
        )

    def arrived(k):
        source = lax.rem(me + count - k, count)
        return pltpu.make_async_remote_copy(
            src_ref=own,
            dst_ref=all_ref.at[source],
            send_sem=s2.at[k],
            recv_sem=r2.at[k],
            device_id=place(source),
            device_id_type=MESH,
        )

    def run(step):
        def loop(k, carry):
            step(k)
            return carry

        lax.fori_loop(1, count, loop, 0)

    run(lambda k: first(k).start())
    land[0] = part_ref[me]
    run(lambda k: first(k).wait_recv())
    raw = jnp.sum(land[...], axis=0)
    lane = lax.broadcasted_iota(jnp.int32, raw.shape, 1)
    logits = jnp.where(lane < CAND * ROT, raw * noise_ref[...], -jnp.inf)
    top = jnp.max(logits, axis=1, keepdims=True)
    grown = jnp.exp(logits - top)
    posterior = grown / jnp.sum(grown, axis=1, keepdims=True)
    post_ref[...] = posterior
    rounded = posterior.astype(BF16).astype(F32)
    own[...] = rounded
    run(lambda k: second(k).start())
    all_ref[me] = rounded
    run(lambda k: arrived(k).wait_recv())
    run(lambda k: first(k).wait_send())
    run(lambda k: second(k).wait_send())


def weights(partial, noise, tomo_axis, cls_axis):
    count = tomo_axis * cls_axis
    dma = pltpu.SemaphoreType.DMA
    tile = partial.shape[1:]
    return pl.pallas_call(
        functools.partial(weights_kernel, tomo_axis, cls_axis),
        out_shape=(
            jax.ShapeDtypeStruct(tile, F32),
            jax.ShapeDtypeStruct(partial.shape, F32),
        ),
        in_specs=[pl.BlockSpec(memory_space=pltpu.VMEM)] * 2,
        out_specs=(pl.BlockSpec(memory_space=pltpu.VMEM),) * 2,
        scratch_shapes=[pltpu.VMEM(tile, F32), pltpu.VMEM(partial.shape, F32)]
        + [dma((count,))] * 4,
        compiler_params=pltpu.CompilerParams(collective_id=2, has_side_effects=True),
        name="weights",
    )(partial, noise)


def sums_kernel(place_ref, slots_ref, codes_ref, weights_ref, wedge_ref, class_ref, wsum_ref, table):
    h, tile = pl.program_id(0), pl.program_id(1)
    particles = codes_ref.shape[0]
    wide = class_ref.shape[0]

    @pl.when((h == 0) & (tile == 0))
    def _():
        local = codes_ref[...] - place_ref[1]
        value = weights_ref[...]
        lane = lax.broadcasted_iota(jnp.int32, (particles, wide), 1)
        total = jnp.zeros((particles, wide), F32)
        for k in range(CAND * ROT):
            total += jnp.where(local[:, k : k + 1] == lane, value[:, k : k + 1], 0.0)
        zero = jnp.zeros((particles // 8, 8, wide), F32)
        stacked = total.reshape(particles // 8, 8, wide)
        first = jnp.concatenate([stacked, zero], axis=1).reshape(2 * particles, wide)
        second = jnp.concatenate([zero, stacked], axis=1).reshape(2 * particles, wide)
        table[0] = first.T.astype(BF16)
        table[1] = second.T.astype(BF16)
        tomos = wedge_ref.shape[0]
        hot = codes_ref[:, CAND * ROT : CAND * ROT + 1] == lax.broadcasted_iota(
            jnp.int32, (particles, tomos), 1
        )
        masks = dot(hot.astype(F32).astype(BF16), wedge_ref[...]).astype(BF16)
        wsum_ref[...] = dot(total.T.astype(BF16), masks)

    lanes = KB * KB // GROUPS
    result = dot(table[h], slots_ref[0])
    for k in range(result.shape[1] // lanes):
        column = pl.multiple_of(k * KB * KB + tile * lanes, lanes)
        class_ref[:, pl.ds(column, lanes)] = result[:, k * lanes : (k + 1) * lanes]


def sums(place, slots, codes, all_weights, wedge_columns, wide):
    rows, step = slots.shape[1:]
    width = step * GROUPS
    return pl.pallas_call(
        sums_kernel,
        grid_spec=pltpu.PrefetchScalarGridSpec(
            num_scalar_prefetch=1,
            grid=(2, GROUPS),
            in_specs=[
                pl.BlockSpec((1, rows, step), lambda h, i, place: (i, 0, 0)),
                pl.BlockSpec(codes.shape, lambda h, i, place: (0, 0)),
                pl.BlockSpec(all_weights.shape, lambda h, i, place: (0, 0)),
                pl.BlockSpec(wedge_columns.shape, lambda h, i, place: (0, 0)),
            ],
            out_specs=[
                pl.BlockSpec((wide, width), lambda h, i, place: (0, h)),
                pl.BlockSpec((wide, wedge_columns.shape[1]), lambda h, i, place: (0, 0)),
            ],
            scratch_shapes=[pltpu.VMEM((2, wide, rows), BF16)],
        ),
        out_shape=(
            jax.ShapeDtypeStruct((wide, 2 * width), F32),
            jax.ShapeDtypeStruct((wide, wedge_columns.shape[1]), F32),
        ),
        compiler_params=pltpu.CompilerParams(vmem_limit_bytes=VMEM_LIMIT),
        name="sums",
    )(place, slots, codes, all_weights, wedge_columns)


def body(
    tomo_axis,
    cls_axis,
    particles,
    inverse_noise,
    tomogram,
    candidates,
    rotations,
    wedge,
    references,
):
    part_count = particles.shape[0]
    class_count = references.shape[0]
    tomo_count = wedge.shape[0]
    wide = class_count * NSET
    blocks = tomo_axis // 2
    per_block = KB // blocks
    half = per_block // 2
    here = lax.axis_index("tomo")
    class_base = lax.axis_index("cls") * wide
    place = jnp.stack([here, class_base]).astype(jnp.int32)

    pair_codes = (candidates[:, :, None] * NSET + rotations[:, None, :]).reshape(part_count, -1)
    code_rows = jnp.concatenate(
        [
            pair_codes,
            tomogram[:, None],
            jnp.zeros((part_count, LANES - CAND * ROT - 1), jnp.int32),
        ],
        axis=1,
    )
    local_hot = (
        (tomogram - here * tomo_count)[:, None] == jnp.arange(tomo_count, dtype=jnp.int32)[None, :]
    ).astype(F32)
    own_masks = jnp.dot(local_hot, wedge.reshape(tomo_count, KB * KB).astype(F32))
    own_masks = own_masks.reshape(part_count, blocks, 2, half, KB).transpose(1, 3, 2, 0, 4)
    mask_rows = jnp.tile(own_masks.reshape(KB * part_count, KB), (1, LANES // KB))

    wedge_own = wedge.reshape(-1, LANES).astype(BF16)
    slots, codes, wedge_rows = spectra_slots(
        particles, mask_rows, code_rows, wedge_own, tomo_axis, cls_axis
    )
    codes = codes.reshape(-1, LANES)
    wedge_rows = wedge_rows.reshape(-1, KB * KB)
    slots = slots.reshape(GROUPS, -1, slots.shape[-1])

    total_tomos = wedge_rows.shape[0]
    wedge_block = lax.dynamic_slice_in_dim(
        wedge_rows, lax.rem(here, blocks) * (per_block * KB), per_block * KB, 1
    ).reshape(total_tomos, per_block, 1, KB)
    wedge_block = jnp.broadcast_to(
        wedge_block, (total_tomos, per_block, LANES // KB, KB)
    ).reshape(total_tomos, per_block * LANES)
    flat_refs = references.reshape(wide, -1)
    partial = scores(place, slots, flat_refs, wedge_block, codes)
    noise = jnp.broadcast_to(inverse_noise[:, None], (part_count, LANES))
    posterior, all_weights = weights(
        partial.reshape(-1, part_count, LANES), noise, tomo_axis, cls_axis
    )
    columns = KB * KB // tomo_axis
    wedge_columns = lax.dynamic_slice_in_dim(wedge_rows, here * columns, columns, 1)
    class_flat, wedge_flat = sums(
        place, slots, codes, all_weights.reshape(-1, LANES), wedge_columns, wide
    )
    return (
        posterior[:, : CAND * ROT],
        class_flat.reshape(class_count, NSET, -1),
        wedge_flat.reshape(class_count, NSET, columns),
    )


def solution(mesh):
    return jax.shard_map(
        functools.partial(body, mesh.shape["tomo"], mesh.shape["cls"]),
        mesh=mesh,
        in_specs=(
            P(("tomo", "cls"), None, None),
            P(("tomo", "cls")),
            P(("tomo", "cls")),
            P(("tomo", "cls"), None),
            P(("tomo", "cls"), None),
            P("tomo", None, None),
            P("cls", None, None),
        ),
        out_specs=(P(("tomo", "cls"), None), P("cls", None, "tomo"), P("cls", None, "tomo")),
        check_vma=False,
    )
```

```python
import functools
import math

import jax
import jax.numpy as jnp
import ml_dtypes
import numpy as np
from jax import lax
from jax.experimental import pallas as pl
from jax.experimental.pallas import tpu as pltpu
from jax.sharding import PartitionSpec as P

KB = 32
NSET = 16
ROT = 8
CAND = 4
LANES = 128
GROUPS = 4
MESH = pl.DeviceIdType.MESH
BF16 = jnp.bfloat16
F32 = jnp.float32
HIGHEST = lax.Precision.HIGHEST
VMEM_LIMIT = 56 * 1024 * 1024


def split_table(table):
    high = table.astype(ml_dtypes.bfloat16)
    low = (table - high.astype(np.float64)).astype(ml_dtypes.bfloat16)
    return high, low


def dft_table(length):
    frequency = np.arange(KB) - KB // 2
    radians = np.mod(np.outer(frequency, np.arange(length)), length) * (2.0 * math.pi / length)
    return np.exp(-1j * radians) / math.sqrt(length)


@functools.lru_cache(maxsize=None)
def plane_tables(length):
    one = dft_table(length)
    plane = np.einsum("jy,kz->yzjk", one, one).reshape(length * length, KB * KB // LANES, LANES)
    both = np.stack([plane.real, plane.imag], axis=2).reshape(length * length, 2 * KB * KB)
    return split_table(both)


@functools.lru_cache(maxsize=None)
def depth_tables(length, part_count, tomo_axis):
    blocks = tomo_axis // 2
    per_block = KB // blocks
    half = per_block // 2
    one = dft_table(length)
    big = np.zeros((2, blocks, half, 2, part_count, part_count, length))
    for block in range(blocks):
        for k in range(half):
            for h in range(2):
                row = one[block * per_block + h * half + k]
                for p in range(part_count):
                    big[0, block, k, h, p, p] = row.real
                    big[1, block, k, h, p, p] = row.imag
    return split_table(big.reshape(2 * KB * part_count, part_count * length))


def dot(a, b):
    return jnp.dot(a, b, preferred_element_type=F32)


def spectra_kernel(
    tomo_axis,
    cls_axis,
    x_ref,
    th_ref,
    tl_ref,
    wh_ref,
    wl_ref,
    mask_ref,
    code_ref,
    wedge_ref,
    out_ref,
    codes_ref,
    wedges_ref,
    m_ref,
    local_sem,
    s1,
    r1,
    sx,
    rx,
    sc,
    rc,
    sk,
    rk,
    sw,
    rw,
):
    tile = pl.program_id(0)
    count = tomo_axis * cls_axis
    blocks = tomo_axis // 2
    half = KB // blocks // 2
    per_group = KB * KB // LANES // GROUPS
    lanes = per_group * LANES
    me_t, me_c = lax.axis_index("tomo"), lax.axis_index("cls")
    mine = me_t * cls_axis + me_c
    x_axis = cls_axis // 2
    xi, core = me_c // 2, me_c % 2
    sibling = (me_t, xi * 2 + 1 - core)

    def x_peer(d):
        return (me_t, lax.rem(xi + d, x_axis) * 2 + core)

    def x_source(d):
        return lax.rem(xi + x_axis - d, x_axis)

    def tomo_source(k):
        return lax.rem(me_t + tomo_axis - k, tomo_axis)

    def remote(src, dst, send, recv, device):
        return pltpu.make_async_remote_copy(
            src_ref=src,
            dst_ref=dst,
            send_sem=send,
            recv_sem=recv,
            device_id=device,
            device_id_type=MESH,
        )

    def device_of(index):
        return (index // cls_axis, lax.rem(index, cls_axis))

    def code_copy(k, slot, device):
        return remote(code_ref, codes_ref.at[slot], sk.at[k], rk.at[k], device)

    def wedge_copy(k, slot, device):
        return remote(wedge_ref, wedges_ref.at[slot], sw.at[k], rw.at[k], device)

    def first(g, k):
        target = lax.rem(me_t + k, tomo_axis)
        return remote(
            m_ref.at[g, target], out_ref.at[g, mine], s1.at[g, k], r1.at[g, k], (target, me_c)
        )

    def first_arrived(g, k):
        slot = tomo_source(k) * cls_axis + me_c
        return remote(
            m_ref.at[g, 0], out_ref.at[g, slot], s1.at[g, k], r1.at[g, k], (tomo_source(k), me_c)
        )

    def across(g, d, k, slot):
        here = out_ref.at[g, slot]
        return remote(here, here, sx.at[g, d, k], rx.at[g, d, k], x_peer(d))

    def over(g, d, k, slot):
        here = out_ref.at[g, slot]
        return remote(here, here, sc.at[g, d, k], rc.at[g, d, k], sibling)

    def own_copy(g):
        return pltpu.make_async_copy(m_ref.at[g, me_t], out_ref.at[g, mine], local_sem.at[g])

    def own_small():
        return (
            pltpu.make_async_copy(code_ref, codes_ref.at[mine], local_sem.at[GROUPS]),
            pltpu.make_async_copy(wedge_ref, wedges_ref.at[me_t], local_sem.at[GROUPS + 1]),
        )

    def run(low, high, step):
        def loop(k, carry):
            step(k)
            return carry

        lax.fori_loop(low, high, loop, 0)

    def send(g):
        own_copy(g).start()
        for k in range(1, tomo_axis):
            first(g, k).start()

    def forward(g):
        for k in range(tomo_axis):
            slot = tomo_source(k) * cls_axis + me_c
            if k == 0:
                own_copy(g).wait()
            else:
                first_arrived(g, k).wait_recv()
            for d in range(1, x_axis):
                across(g, d, k, slot).start()
            over(g, 0, k, slot).start()

    def share(g):
        for k in range(tomo_axis):
            for d in range(1, x_axis):
                slot = tomo_source(k) * cls_axis + x_source(d) * 2 + core
                across(g, d, k, slot).wait_recv()
                over(g, d, k, slot).start()

    @pl.when(tile == 0)
    def _():
        barrier = pltpu.get_barrier_semaphore()
        run(
            1,
            count,
            lambda k: pl.semaphore_signal(
                barrier, inc=1, device_id=device_of(lax.rem(mine + k, count)), device_id_type=MESH
            ),
        )
        pl.semaphore_wait(barrier, count - 1)
        for one in own_small():
            one.start()
        for k in range(1, tomo_axis):
            wedge_copy(k, me_t, (lax.rem(me_t + k, tomo_axis), me_c)).start()
        run(1, count, lambda k: code_copy(k, mine, device_of(lax.rem(mine + k, count))).start())

    values = x_ref[...]
    plane = dot(values, th_ref[...]) + dot(values, tl_ref[...])
    high = plane.astype(BF16)
    low = (plane - high.astype(F32)).astype(BF16)
    wide = dot(wh_ref[...], high) + dot(wh_ref[...], low) + dot(wl_ref[...], high)
    rows = wide.shape[0] // 2
    mask = mask_ref[...]
    real = (wide[:rows, :LANES] - wide[rows:, LANES:]) * mask
    imag = (wide[:rows, LANES:] + wide[rows:, :LANES]) * mask
    height = rows // (blocks * half)
    at = tile // per_group
    offset = lax.rem(tile, per_group) * LANES
    for a, part in enumerate((real.astype(BF16), imag.astype(BF16))):
        for block in range(blocks):
            for k in range(half):
                start = (block * half + k) * height
                column = pl.multiple_of(k * lanes + offset, LANES)
                m_ref[at, a * blocks + block, :, pl.ds(column, LANES)] = part[
                    start : start + height
                ]

    for g in range(GROUPS):

        @pl.when(tile == (g + 1) * per_group - 1)
        def _(g=g):
            send(g)
            if g >= 1:
                forward(g - 1)
            if g >= 2:
                share(g - 2)

    @pl.when(tile == GROUPS * per_group - 1)
    def _():
        if GROUPS >= 2:
            share(GROUPS - 2)
        forward(GROUPS - 1)
        share(GROUPS - 1)
        for g in range(GROUPS):
            for k in range(tomo_axis):
                for d in range(x_axis):
                    slot = tomo_source(k) * cls_axis + x_source(d) * 2 + 1 - core
                    over(g, d, k, slot).wait_recv()
        for one in own_small():
            one.wait()
        for k in range(1, tomo_axis):
            wedge_copy(k, tomo_source(k), (tomo_source(k), me_c)).wait_recv()

        def code_arrived(k):
            source = lax.rem(mine + count - k, count)
            code_copy(k, source, device_of(source)).wait_recv()

        run(1, count, code_arrived)
        run(1, count, lambda k: code_copy(k, mine, device_of(lax.rem(mine + k, count))).wait_send())
        for k in range(1, tomo_axis):
            wedge_copy(k, me_t, (lax.rem(me_t + k, tomo_axis), me_c)).wait_send()
        for g in range(GROUPS):
            for k in range(tomo_axis):
                if k:
                    first(g, k).wait_send()
                for d in range(x_axis):
                    slot = tomo_source(k) * cls_axis + x_source(d) * 2 + core
                    if d:
                        across(g, d, k, tomo_source(k) * cls_axis + me_c).wait_send()
                    over(g, d, k, slot).wait_send()


def spectra_slots(particles, mask_rows, code_rows, wedge_own, tomo_axis, cls_axis):
    part_count, length, plane_size = particles.shape
    count = tomo_axis * cls_axis
    x_axis = cls_axis // 2
    half = KB // tomo_axis
    piece = half * KB * KB // GROUPS
    th, tl = plane_tables(length)
    wh, wl = depth_tables(length, part_count, tomo_axis)
    tiles = KB * KB // LANES
    dma = pltpu.SemaphoreType.DMA
    whole = lambda shape: pl.BlockSpec(shape, lambda j: (0,) * len(shape))
    return pl.pallas_call(
        functools.partial(spectra_kernel, tomo_axis, cls_axis),
        grid=(tiles,),
        out_shape=(
            jax.ShapeDtypeStruct((GROUPS, count, 2 * part_count, piece), BF16),
            jax.ShapeDtypeStruct((count,) + code_rows.shape, jnp.int32),
            jax.ShapeDtypeStruct((tomo_axis,) + wedge_own.shape, BF16),
        ),
        in_specs=[
            whole((part_count * length, plane_size)),
            pl.BlockSpec((plane_size, 2 * LANES), lambda j: (0, j)),
            pl.BlockSpec((plane_size, 2 * LANES), lambda j: (0, j)),
            whole(wh.shape),
            whole(wl.shape),
            whole(mask_rows.shape),
            pl.BlockSpec(memory_space=pl.ANY),
            pl.BlockSpec(memory_space=pl.ANY),
        ],
        out_specs=(pl.BlockSpec(memory_space=pl.ANY),) * 3,
        scratch_shapes=[
            pltpu.VMEM((GROUPS, tomo_axis, 2 * part_count, piece), BF16),
            dma((GROUPS + 2,)),
            dma((GROUPS, tomo_axis)),
            dma((GROUPS, tomo_axis)),
            dma((GROUPS, x_axis, tomo_axis)),
            dma((GROUPS, x_axis, tomo_axis)),
            dma((GROUPS, x_axis, tomo_axis)),
            dma((GROUPS, x_axis, tomo_axis)),
            dma((count,)),
            dma((count,)),
            dma((tomo_axis,)),
            dma((tomo_axis,)),
        ],
        compiler_params=pltpu.CompilerParams(
            collective_id=1, has_side_effects=True, vmem_limit_bytes=VMEM_LIMIT
        ),
        name="spectra",
    )(
        particles.reshape(part_count * length, plane_size),
        jnp.asarray(th),
        jnp.asarray(tl),
        jnp.asarray(wh),
        jnp.asarray(wl),
        mask_rows,
        code_rows,
        wedge_own,
    )


def score_kernel(place_ref, slots_ref, refs_ref, wedge_ref, codes_ref, out_ref, acc, pen):
    h = pl.program_id(0)
    refs = refs_ref[...]
    products = None
    lanes = KB * KB // GROUPS
    for g in range(GROUPS):
        columns = jnp.concatenate(
            [
                refs[:, k * KB * KB + g * lanes : k * KB * KB + (g + 1) * lanes]
                for k in range(refs.shape[1] // (KB * KB))
            ],
            axis=1,
        )
        term = lax.dot_general(
            slots_ref[g], columns, (((1,), (1,)), ((), ())), preferred_element_type=F32
        )
        products = term if products is None else products + term
    rows, wide = products.shape
    paired = products.reshape(rows // 16, 16, wide)
    inner = jnp.where(h == 0, paired[:, :8], paired[:, 8:]).reshape(rows // 2, wide)
    pieces = []
    plane = KB * KB
    for k in range(refs.shape[1] // plane):
        total = None
        for j in range(plane // LANES):
            start = k * plane + j * LANES
            piece = refs[:, start : start + LANES].astype(F32)
            square = piece * piece
            total = square if total is None else total + square
        pieces.append(total)
    power = jnp.concatenate(pieces, axis=1)
    penalty = lax.dot_general(
        wedge_ref[...].astype(F32),
        power,
        (((1,), (1,)), ((), ())),
        preferred_element_type=F32,
        precision=HIGHEST,
    )

    @pl.when(h == 0)
    def _():
        acc[...] = inner
        pen[...] = penalty

    @pl.when(h == 1)
    def _():
        codes = codes_ref[...]
        tomos = pen.shape[0]
        hot = codes[:, CAND * ROT : CAND * ROT + 1] == lax.broadcasted_iota(
            jnp.int32, (rows // 2, tomos), 1
        )
        chosen = jnp.dot(
            hot.astype(F32), pen[...] + penalty, preferred_element_type=F32, precision=HIGHEST
        )
        raw = acc[...] + inner - 0.5 * chosen
        local = codes - place_ref[1]
        lane = lax.broadcasted_iota(jnp.int32, codes.shape, 1)
        valid = (local >= 0) & (local < wide) & (lane < CAND * ROT)
        picked = jnp.take_along_axis(raw, jnp.where(valid, local, 0), axis=1)
        out_ref[...] = jnp.where(valid, picked, 0.0)


def scores(place, slots, refs, wedge_block, codes):
    rows, width = slots.shape[1], slots.shape[2] * GROUPS
    tomos = wedge_block.shape[0]
    depth = wedge_block.shape[1] // 2
    wide = refs.shape[0]
    return pl.pallas_call(
        score_kernel,
        grid_spec=pltpu.PrefetchScalarGridSpec(
            num_scalar_prefetch=1,
            grid=(2,),
            in_specs=[
                pl.BlockSpec(slots.shape, lambda h, place: (0, 0, 0)),
                pl.BlockSpec((wide, width), lambda h, place: (0, 2 * place[0] + h)),
                pl.BlockSpec((tomos, depth), lambda h, place: (0, h)),
                pl.BlockSpec(codes.shape, lambda h, place: (0, 0)),
            ],
            out_specs=pl.BlockSpec(codes.shape, lambda h, place: (0, 0)),
            scratch_shapes=[
                pltpu.VMEM((rows // 2, wide), F32),
                pltpu.VMEM((tomos, wide), F32),
            ],
        ),
        out_shape=jax.ShapeDtypeStruct(codes.shape, F32),
        compiler_params=pltpu.CompilerParams(vmem_limit_bytes=VMEM_LIMIT),
        name="scores",
    )(place, slots, refs, wedge_block, codes)


def weights_kernel(
    tomo_axis, cls_axis, part_ref, noise_ref, post_ref, all_ref, own, land, s1, r1, s2, r2
):
    count = tomo_axis * cls_axis
    me_t, me_c = lax.axis_index("tomo"), lax.axis_index("cls")
    me = me_t * cls_axis + me_c

    def place(index):
        return (index // cls_axis, lax.rem(index, cls_axis))

    barrier = pltpu.get_barrier_semaphore()

    def greet(k, carry):
        pl.semaphore_signal(
            barrier, inc=1, device_id=place(lax.rem(me + k, count)), device_id_type=MESH
        )
        return carry

    lax.fori_loop(1, count, greet, 0)
    pl.semaphore_wait(barrier, count - 1)

    def first(k):
        target = lax.rem(me + k, count)
        return pltpu.make_async_remote_copy(
            src_ref=part_ref.at[target],
            dst_ref=land.at[k],
            send_sem=s1.at[k],
            recv_sem=r1.at[k],
            device_id=place(target),
            device_id_type=MESH,
        )

    def second(k):
        target = lax.rem(me + k, count)
        return pltpu.make_async_remote_copy(
            src_ref=own,
            dst_ref=all_ref.at[me],
            send_sem=s2.at[k],
            recv_sem=r2.at[k],
            device_id=place(target),
            device_id_type=MESH,
        )

    def arrived(k):
        source = lax.rem(me + count - k, count)
        return pltpu.make_async_remote_copy(
            src_ref=own,
            dst_ref=all_ref.at[source],
            send_sem=s2.at[k],
            recv_sem=r2.at[k],
            device_id=place(source),
            device_id_type=MESH,
        )

    def run(step):
        def loop(k, carry):
            step(k)
            return carry

        lax.fori_loop(1, count, loop, 0)

    run(lambda k: first(k).start())
    land[0] = part_ref[me]
    run(lambda k: first(k).wait_recv())
    raw = jnp.sum(land[...], axis=0)
    lane = lax.broadcasted_iota(jnp.int32, raw.shape, 1)
    logits = jnp.where(lane < CAND * ROT, raw * noise_ref[...], -jnp.inf)
    top = jnp.max(logits, axis=1, keepdims=True)
    grown = jnp.exp(logits - top)
    posterior = grown / jnp.sum(grown, axis=1, keepdims=True)
    post_ref[...] = posterior
    rounded = posterior.astype(BF16).astype(F32)
    own[...] = rounded
    run(lambda k: second(k).start())
    all_ref[me] = rounded
    run(lambda k: arrived(k).wait_recv())
    run(lambda k: first(k).wait_send())
    run(lambda k: second(k).wait_send())


def weights(partial, noise, tomo_axis, cls_axis):
    count = tomo_axis * cls_axis
    dma = pltpu.SemaphoreType.DMA
    tile = partial.shape[1:]
    return pl.pallas_call(
        functools.partial(weights_kernel, tomo_axis, cls_axis),
        out_shape=(
            jax.ShapeDtypeStruct(tile, F32),
            jax.ShapeDtypeStruct(partial.shape, F32),
        ),
        in_specs=[pl.BlockSpec(memory_space=pltpu.VMEM)] * 2,
        out_specs=(pl.BlockSpec(memory_space=pltpu.VMEM),) * 2,
        scratch_shapes=[pltpu.VMEM(tile, F32), pltpu.VMEM(partial.shape, F32)]
        + [dma((count,))] * 4,
        compiler_params=pltpu.CompilerParams(collective_id=2, has_side_effects=True),
        name="weights",
    )(partial, noise)


def sums_kernel(place_ref, slots_ref, codes_ref, weights_ref, wedge_ref, class_ref, wsum_ref, table):
    k_block, h = pl.program_id(0), pl.program_id(1)
    particles = codes_ref.shape[0]
    wide = class_ref.shape[0]

    @pl.when((h == 0) & (k_block == 0))
    def _():
        local = codes_ref[...] - place_ref[1]
        value = weights_ref[...]
        lane = lax.broadcasted_iota(jnp.int32, (particles, wide), 1)
        total = jnp.zeros((particles, wide), F32)
        for k in range(CAND * ROT):
            total += jnp.where(local[:, k : k + 1] == lane, value[:, k : k + 1], 0.0)
        zero = jnp.zeros((particles // 8, 8, wide), F32)
        stacked = total.reshape(particles // 8, 8, wide)
        first = jnp.concatenate([stacked, zero], axis=1).reshape(2 * particles, wide)
        second = jnp.concatenate([zero, stacked], axis=1).reshape(2 * particles, wide)
        table[0] = first.T.astype(BF16)
        table[1] = second.T.astype(BF16)
        tomos = wedge_ref.shape[0]
        hot = codes_ref[:, CAND * ROT : CAND * ROT + 1] == lax.broadcasted_iota(
            jnp.int32, (particles, tomos), 1
        )
        masks = dot(hot.astype(F32).astype(BF16), wedge_ref[...]).astype(BF16)
        wsum_ref[...] = dot(total.T.astype(BF16), masks)

    lanes = slots_ref.shape[2]
    for g in range(GROUPS):
        class_ref[:, g * lanes : (g + 1) * lanes] = dot(table[h], slots_ref[g])


def sums(place, slots, codes, all_weights, wedge_columns, wide):
    rows, step = slots.shape[1:]
    width = step * GROUPS
    lanes = KB * KB // GROUPS
    half = step // lanes
    return pl.pallas_call(
        sums_kernel,
        grid_spec=pltpu.PrefetchScalarGridSpec(
            num_scalar_prefetch=1,
            grid=(half, 2),
            in_specs=[
                pl.BlockSpec((GROUPS, rows, lanes), lambda i, h, place: (0, 0, i)),
                pl.BlockSpec(codes.shape, lambda h, i, place: (0, 0)),
                pl.BlockSpec(all_weights.shape, lambda h, i, place: (0, 0)),
                pl.BlockSpec(wedge_columns.shape, lambda h, i, place: (0, 0)),
            ],
            out_specs=[
                pl.BlockSpec((wide, KB * KB), lambda i, h, place: (0, h * half + i)),
                pl.BlockSpec((wide, wedge_columns.shape[1]), lambda h, i, place: (0, 0)),
            ],
            scratch_shapes=[pltpu.VMEM((2, wide, rows), BF16)],
        ),
        out_shape=(
            jax.ShapeDtypeStruct((wide, 2 * width), F32),
            jax.ShapeDtypeStruct((wide, wedge_columns.shape[1]), F32),
        ),
        compiler_params=pltpu.CompilerParams(vmem_limit_bytes=VMEM_LIMIT),
        name="sums",
    )(place, slots, codes, all_weights, wedge_columns)


def body(
    tomo_axis,
    cls_axis,
    particles,
    inverse_noise,
    tomogram,
    candidates,
    rotations,
    wedge,
    references,
):
    part_count = particles.shape[0]
    class_count = references.shape[0]
    tomo_count = wedge.shape[0]
    wide = class_count * NSET
    blocks = tomo_axis // 2
    per_block = KB // blocks
    half = per_block // 2
    here = lax.axis_index("tomo")
    class_base = lax.axis_index("cls") * wide
    place = jnp.stack([here, class_base]).astype(jnp.int32)

    pair_codes = (candidates[:, :, None] * NSET + rotations[:, None, :]).reshape(part_count, -1)
    code_rows = jnp.concatenate(
        [
            pair_codes,
            tomogram[:, None],
            jnp.zeros((part_count, LANES - CAND * ROT - 1), jnp.int32),
        ],
        axis=1,
    )
    local_hot = (
        (tomogram - here * tomo_count)[:, None] == jnp.arange(tomo_count, dtype=jnp.int32)[None, :]
    ).astype(F32)
    own_masks = jnp.dot(local_hot, wedge.reshape(tomo_count, KB * KB).astype(F32))
    own_masks = own_masks.reshape(part_count, blocks, 2, half, KB).transpose(1, 3, 2, 0, 4)
    mask_rows = jnp.tile(own_masks.reshape(KB * part_count, KB), (1, LANES // KB))

    wedge_own = wedge.reshape(-1, LANES).astype(BF16)
    slots, codes, wedge_rows = spectra_slots(
        particles, mask_rows, code_rows, wedge_own, tomo_axis, cls_axis
    )
    codes = codes.reshape(-1, LANES)
    wedge_rows = wedge_rows.reshape(-1, KB * KB)
    slots = slots.reshape(GROUPS, -1, slots.shape[-1])

    total_tomos = wedge_rows.shape[0]
    wedge_block = lax.dynamic_slice_in_dim(
        wedge_rows, lax.rem(here, blocks) * (per_block * KB), per_block * KB, 1
    ).reshape(total_tomos, per_block, 1, KB)
    wedge_block = jnp.broadcast_to(
        wedge_block, (total_tomos, per_block, LANES // KB, KB)
    ).reshape(total_tomos, per_block * LANES)
    flat_refs = references.reshape(wide, -1)
    partial = scores(place, slots, flat_refs, wedge_block, codes)
    noise = inverse_noise[:, None]
    posterior, all_weights = weights(
        partial.reshape(-1, part_count, LANES), noise, tomo_axis, cls_axis
    )
    columns = KB * KB // tomo_axis
    wedge_columns = lax.dynamic_slice_in_dim(wedge_rows, here * columns, columns, 1)
    class_flat, wedge_flat = sums(
        place, slots, codes, all_weights.reshape(-1, LANES), wedge_columns, wide
    )
    return (
        posterior[:, : CAND * ROT],
        class_flat.reshape(class_count, NSET, -1),
        wedge_flat.reshape(class_count, NSET, columns),
    )


def solution(mesh):
    return jax.shard_map(
        functools.partial(body, mesh.shape["tomo"], mesh.shape["cls"]),
        mesh=mesh,
        in_specs=(
            P(("tomo", "cls"), None, None),
            P(("tomo", "cls")),
            P(("tomo", "cls")),
            P(("tomo", "cls"), None),
            P(("tomo", "cls"), None),
            P("tomo", None, None),
            P("cls", None, None),
        ),
        out_specs=(P(("tomo", "cls"), None), P("cls", None, "tomo"), P("cls", None, "tomo")),
        check_vma=False,
    )
```
